128 devices in a mesh: dp: 8 (over z, core), tensor: 16 (over x, y).
Axes of the slice: x: 4, y: 4, z: 4, core: 2. Of those that a mesh axis runs over, the one named last changes fastest.
Arguments:
- tokens: bfloat16 [4096, 4096], P('dp', 'tensor'), may hold values from -10 to 10
- out_grad: bfloat16 [4096, 4096], P('dp', 'tensor'), may hold values from -10 to 10
- gate_weight: bfloat16 [4096, 12288], P(None, 'tensor'), may hold values from -0.09375 to 0.09375
- up_weight: bfloat16 [4096, 12288], P(None, 'tensor'), may hold values from -0.09375 to 0.09375
- down_weight: bfloat16 [12288, 4096], P('tensor'), may hold values from -0.0546875 to 0.0546875
- slot_ffn_block: int32 [768], P('tensor'), may hold values from 0 to 5
- slot_model_block: int32 [768], P('tensor'), may hold values from 0 to 31
- slot_kind: int32 [768], P('tensor'), may hold values from 0 to 2
- live_count: int32 [16], P('tensor'), may hold values from 1 to 48, as said below
Outputs:
- input_grad: bfloat16 [4096, 4096], P('dp', 'tensor')
- block_grads: float32 [768, 128, 128], P('tensor', 'dp')
The draws below stay inside these ranges and needn't reach their ends.
Inputs may be any that keep to these rules, and one draw needn't show every extreme that they name: Slots of holder h are 0 to live_count[h] - 1 in its 48 slots; some holder uses all 48.
All inputs are finite; a program needn't handle non-finite values.
Results may differ from the reference program's by a relative error of at most 0.019.
Values may be sent and summed in bfloat16 or wider, within the bound.
A program may use at most 128 MiB of HBM per device.

```python
import math
import jax
import jax.numpy as jnp
from jax import lax

D = 4096
FF = 12288
TILE = 128
LEN = 128
CAP = 48
SEQS = 32
TOKENS = 4096
DB = 32
FB_DEV = 6
SLOTS = 768
N_TENSOR = 16


def sequence_scales(key):
    order_key = jax.random.fold_in(key, 5)
    ranks = jax.random.permutation(order_key, SEQS)
    spread = ranks.astype(jnp.float32) / max(SEQS - 1, 1)
    return jnp.exp(-0.9 + 1.8 * spread)


def draw_tokens(key, part):
    scales = sequence_scales(key)
    key = jax.random.fold_in(key, 11)
    values = jax.random.truncated_normal(key, -4.0, 4.0, (TOKENS, D), jnp.float32)
    return (values * jnp.repeat(scales, LEN)[:, None]).astype(jnp.bfloat16)


def draw_out_grad(key, part):
    scales = sequence_scales(key)
    key = jax.random.fold_in(key, 13)
    values = jax.random.truncated_normal(key, -4.0, 4.0, (TOKENS, D), jnp.float32)
    return (values * jnp.repeat(scales, LEN)[:, None]).astype(jnp.bfloat16)


def draw_live_count(key, part):
    key = jax.random.fold_in(key, 7)
    key_one, key_two = jax.random.split(key)
    counts = jax.random.randint(key_one, (N_TENSOR,), max(1, CAP // 3), CAP + 1)
    full_at = jax.random.randint(key_two, (), 0, N_TENSOR)
    return jnp.where(jnp.arange(N_TENSOR) == full_at, CAP, counts).astype(jnp.int32)


def plant(drawn, key, low, largest):
    extent = drawn.shape
    index_at = [jax.random.randint(jax.random.fold_in(key, axis), (), 0, extent[axis]) for axis in range(len(extent))]
    drawn = drawn.at[tuple(index_at)].set(low)
    longest = extent.index(max(extent))
    index_at[longest] = (index_at[longest] + 1) % extent[longest]
    return drawn.at[tuple(index_at)].set(largest)


def steps_of(key, shape, cuts, least, largest):
    def one(axis_at, shards_of):
        steps = jax.random.uniform(jax.random.fold_in(jax.random.fold_in(key, 6), axis_at), (shards_of,), jnp.float32, least / len(cuts), largest / len(cuts))
        return jnp.repeat(jnp.exp(steps), shape[axis_at] // shards_of).reshape((-1,) + (1,) * (len(shape) - axis_at - 1))

    level = one(*cuts[0])
    for cut in cuts[1:]:
        level = level * one(*cut)
    return level


def gaussian(stream_key, extent, width, reach, cuts=(), kind=jnp.bfloat16):
    drawn = jax.random.normal(stream_key, extent, jnp.float32) * width
    if len(cuts) > 0:
        drawn = steps_of(stream_key, extent, cuts, -0.22, 0.18) * drawn
    return jnp.clip(drawn, min=-reach, max=reach).astype(kind)


def setup_inputs(seed: int = 0) -> dict:
    streams_of = jax.random.split(jax.random.key(seed), 10)
    return {
        "tokens": draw_tokens(jax.random.fold_in(streams_of[9], 71), 0),
        "out_grad": draw_out_grad(jax.random.fold_in(streams_of[9], 71), 0),
        "gate_weight": gaussian(streams_of[2], (D, FF), D ** -0.5, 0.09375, ((1, 16),)),
        "up_weight": gaussian(streams_of[3], (D, FF), D ** -0.5, 0.09375, ((1, 16),)),
        "down_weight": gaussian(streams_of[4], (FF, D), FF ** -0.5, 0.0546875, ((0, 16),)),
        "slot_ffn_block": plant(jax.random.randint(streams_of[5], (SLOTS,), 0, FB_DEV), jax.random.fold_in(streams_of[5], 1), 0, FB_DEV - 1).astype(jnp.int32),
        "slot_model_block": plant(jax.random.randint(streams_of[6], (SLOTS,), 0, DB), jax.random.fold_in(streams_of[6], 1), 0, DB - 1).astype(jnp.int32),
        "slot_kind": plant(jax.random.randint(streams_of[7], (SLOTS,), 0, 3), jax.random.fold_in(streams_of[7], 1), 0, 2).astype(jnp.int32),
        "live_count": draw_live_count(jax.random.fold_in(streams_of[9], 71), 0),
    }


def reference(tokens, out_grad, gate_weight, up_weight, down_weight, slot_ffn_block, slot_model_block, slot_kind, live_count):
    gate_pre = jnp.dot(tokens, gate_weight, preferred_element_type=jnp.float32)
    up_proj = jnp.dot(tokens, up_weight, preferred_element_type=jnp.float32)
    sigmoid_gate = jax.nn.sigmoid(gate_pre)
    hidden = (gate_pre * sigmoid_gate * up_proj).astype(jnp.bfloat16)
    hidden_grad = jnp.dot(out_grad, down_weight.T, preferred_element_type=jnp.float32)
    grad_gate = (hidden_grad * up_proj * sigmoid_gate * (1.0 + gate_pre * (1.0 - sigmoid_gate))).astype(jnp.bfloat16)
    grad_up = (hidden_grad * gate_pre * sigmoid_gate).astype(jnp.bfloat16)
    group_units = FB_DEV * TILE
    group_count = FF // group_units

    def by_group(matrix):
        return matrix.reshape(matrix.shape[0], group_count, group_units).transpose(1, 0, 2)

    def add_group(carry, pieces):
        gg_part, gu_part, gw_part, uw_part = pieces
        partial_value = (jnp.dot(gg_part, gw_part.T, preferred_element_type=jnp.float32) + jnp.dot(gu_part, uw_part.T, preferred_element_type=jnp.float32)).astype(jnp.bfloat16)
        partial_value = lax.optimization_barrier(partial_value)
        return (carry + partial_value.astype(jnp.float32), None)
    dx_total, unused_out = lax.scan(add_group, jnp.zeros((TOKENS, D), jnp.float32), (by_group(grad_gate), by_group(grad_up), by_group(gate_weight), by_group(up_weight)))
    input_grad = dx_total.astype(jnp.bfloat16)
    slot_ids = jnp.arange(SLOTS, dtype=jnp.int32)
    holder = slot_ids // CAP
    ffn_global = holder * FB_DEV + slot_ffn_block
    live_slot = (slot_ids % CAP < live_count[holder]).astype(jnp.float32)
    x_blocks = tokens.reshape(SEQS, LEN, DB, TILE)
    g_blocks = out_grad.reshape(SEQS, LEN, DB, TILE)
    h_blocks = hidden.reshape(SEQS, LEN, FF // TILE, TILE)
    gg_blocks = grad_gate.reshape(SEQS, LEN, FF // TILE, TILE)
    gu_blocks = grad_up.reshape(SEQS, LEN, FF // TILE, TILE)
    kinds = slot_kind[None, :, None]

    def seq_tiles(index):
        x_cols = x_blocks[index][:, slot_model_block]
        g_cols = g_blocks[index][:, slot_model_block]
        h_cols = h_blocks[index][:, ffn_global]
        gg_cols = gg_blocks[index][:, ffn_global]
        gu_cols = gu_blocks[index][:, ffn_global]
        left_cols = jnp.where(kinds == 2, h_cols, x_cols).astype(jnp.float32)
        right_cols = jnp.where(kinds == 0, gg_cols, jnp.where(kinds == 1, gu_cols, g_cols)).astype(jnp.float32)
        block_tiles = jnp.einsum('lci,lcj->cij', left_cols, right_cols)
        return block_tiles * live_slot[:, None, None]

    def seq_square(index):
        block_tiles = seq_tiles(index)
        return jnp.sum(block_tiles * block_tiles)
    square_sum = lax.map(seq_square, jnp.arange(SEQS, dtype=jnp.int32))
    bound = 0.33 * TILE * math.sqrt(LEN * SLOTS)
    clip = jnp.minimum(1.0, bound / jnp.sqrt(square_sum + 1e-06))

    def add_seq(carry, index):
        return (carry + clip[index] * seq_tiles(index), None)
    block_grads, unused = lax.scan(add_seq, jnp.zeros((SLOTS, TILE, TILE), jnp.float32), jnp.arange(SEQS, dtype=jnp.int32))
    return (input_grad, block_grads)
```

```python
import math

import jax
import jax.numpy as jnp
from jax import lax
from jax.experimental import pallas as pl
from jax.experimental.pallas import tpu as pltpu
from jax.sharding import PartitionSpec as P

TILE = 128
LEN = 128
ROWS = 256
SLOTS = 48
NX = 4
XB, GB, HB, GGB, GUB = 0, 32, 64, 70, 76
BLOCKS = 82
OFF = (0, -1, 1, 2)
OFF2 = (2, 1, -1, 0)
MESH = pl.DeviceIdType.MESH
BOUND = 0.33 * TILE * math.sqrt(LEN * 768)
NT = (((1,), (1,)), ((), ()))
TN = (((0,), (0,)), ((), ()))
DPG = 3
DPS = SLOTS // DPG


def mod4(v):
    return lax.rem(v + 8, 4)


def kernel(
    tok,
    og,
    gw,
    uw,
    dw,
    sf,
    sm,
    sk,
    lc,
    out_x,
    out_b,
    cat0,
    cat1,
    wg,
    wu,
    wd,
    acc_g,
    acc_u,
    acc_h,
    p0,
    p1,
    r1,
    r2,
    r3,
    r4,
    tiles,
    nr,
    ssum,
    cr,
    zs,
    zr,
    own_sem,
    w_sem,
    ag_s,
    ag_r,
    rs_s,
    rs_r,
    nr_s,
    nr_r,
    c_s,
    c_r,
    z_s,
    z_r,
):
    dp = lax.axis_index("dp")
    me = lax.axis_index("tensor")
    cx, cy = me // 4, lax.rem(me, 4)
    cz, cc = dp // 2, lax.rem(dp, 2)
    cats = (cat0, cat1)
    ps = (p0, p1)
    sends = []

    own = []
    for h in range(2):
        for arr, src in ((0, tok), (1, og)):
            for k in range(2):
                c = pltpu.make_async_copy(
                    src.at[pl.ds(h * ROWS, ROWS), pl.ds(k * TILE, TILE)],
                    cats[h].at[32 * arr + 2 * me + k],
                    own_sem.at[h, arr, k],
                )
                c.start()
                own.append(c)
    wcopies = [
        pltpu.make_async_copy(gw, wg, w_sem.at[0]),
        pltpu.make_async_copy(uw, wu, w_sem.at[1]),
    ] + [
        pltpu.make_async_copy(dw.at[:, pl.ds(1024 * i, 1024)], wd.at[i], w_sem.at[2 + i])
        for i in range(4)
    ]
    for c in wcopies:
        c.start()

    barrier = pltpu.get_barrier_semaphore()
    for k in range(1, 16):
        pl.semaphore_signal(
            barrier, inc=1, device_id=(dp, lax.rem(me + k, 16)), device_id_type=MESH
        )
    pl.semaphore_signal(barrier, inc=1, device_id=(cz * 2 + 1 - cc, me), device_id_type=MESH)
    for k in range(1, 4):
        pl.semaphore_signal(
            barrier, inc=1, device_id=(mod4(cz + k) * 2 + cc, me), device_id_type=MESH
        )
    pl.semaphore_wait(barrier, 19)

    def rcopy(src, dst, ssem, rsem, dev):
        return pltpu.make_async_remote_copy(
            src_ref=src, dst_ref=dst, send_sem=ssem, recv_sem=rsem, device_id=dev, device_id_type=MESH
        )

    def send(src, dst, ssem, rsem, dev):
        c = rcopy(src, dst, ssem, rsem, dev)
        c.start()
        sends.append(c)

    def tensor_at(first_is_x, a1, a2):
        return a1 * 4 + a2 if first_is_x else a2 * 4 + a1

    def ag(h, arr):
        fx = arr == 0
        c1, c2 = (cx, cy) if fx else (cy, cx)

        def dev(d1, d2):
            return (dp, tensor_at(fx, mod4(c1 + d1), mod4(c2 + d2)))

        def region(d1, d2, part):
            t = tensor_at(fx, mod4(c1 + d1), mod4(c2 + d2))
            rows = (pl.ds(0, ROWS), pl.ds(0, ROWS // 2), pl.ds(ROWS // 2, ROWS // 2))[part]
            return cats[h].at[pl.ds(32 * arr + 2 * t, 2), rows, :]

        def put(idx, d1, d2, part, e1, e2):
            r = region(d1, d2, part)
            send(r, r, ag_s.at[h, arr, idx], ag_r.at[h, arr, idx], dev(e1, e2))

        def got(idx, d1, d2, part):
            r = region(d1, d2, part)
            rcopy(r, r, ag_s.at[h, arr, idx], ag_r.at[h, arr, idx], dev(1, 0)).wait_recv()

        def start():
            put(0, 0, 0, 0, 1, 0)
            put(1, 0, 0, 0, -1, 0)
            put(4, 0, 0, 0, 0, 1)
            put(5, 0, 0, 0, 0, -1)

        def spread(j):
            put(4 + 4 * j, OFF[j], 0, 0, 0, 1)
            put(5 + 4 * j, OFF[j], 0, 0, 0, -1)

        def e1():
            got(0, -1, 0, 0)
            put(2, -1, 0, 1, 1, 0)
            spread(1)

        def e2():
            got(1, 1, 0, 0)
            put(3, 1, 0, 2, -1, 0)
            spread(2)

        def e3():
            got(2, 2, 0, 1)
            got(3, 2, 0, 2)
            spread(3)

        def e4(j):
            got(4 + 4 * j, OFF[j], -1, 0)
            put(6 + 4 * j, OFF[j], -1, 1, 0, 1)
            got(5 + 4 * j, OFF[j], 1, 0)
            put(7 + 4 * j, OFF[j], 1, 2, 0, -1)

        def e5(j):
            got(6 + 4 * j, OFF[j], 2, 1)
            got(7 + 4 * j, OFF[j], 2, 2)

        return start, e1, e2, e3, e4, e5

    AG = [[ag(h, arr) for arr in range(2)] for h in range(2)]

    def ag_step(h, k, *a):
        for arr in range(2):
            AG[h][arr][k](*a)

    def fwd(h, off):
        cat = cats[h]
        yy, xx = mod4(cy + off), mod4(cx + off)

        def body(n, _):
            cols = pl.ds(pl.multiple_of(n * 256, 256), 256)
            lhs = jnp.concatenate(
                [cat[2 * (4 * i + yy) + k] for i in range(4) for k in range(2)], axis=1
            )
            for w, acc in ((wg, acc_g), (wu, acc_u)):
                rhs = jnp.concatenate([w[4 * i + yy, :, cols] for i in range(4)], axis=0)
                v = jnp.dot(lhs, rhs, preferred_element_type=jnp.float32)
                for k in range(2):
                    vk = v[:, k * TILE : (k + 1) * TILE]
                    acc[2 * n + k] = vk if off == 0 else acc[2 * n + k] + vk
            lhs = jnp.concatenate([cat[GB + 8 * xx + k] for k in range(8)], axis=1)
            v = lax.dot_general(lhs, wd[xx, cols, :], NT, preferred_element_type=jnp.float32)
            for k in range(2):
                vk = v[:, k * TILE : (k + 1) * TILE]
                acc_h[2 * n + k] = vk if off == 0 else acc_h[2 * n + k] + vk
            return 0

        lax.fori_loop(0, 3, body, 0)

    def pointwise(h):
        cat = cats[h]

        def body(f, _):
            for r in range(4):
                rows = pl.ds(r * 64, 64)
                g, u, hg = acc_g[f, rows, :], acc_u[f, rows, :], acc_h[f, rows, :]
                s = 1.0 / (1.0 + jnp.exp(-g))
                gs = g * s
                cat[HB + f, rows, :] = (gs * u).astype(jnp.bfloat16)
                cat[GGB + f, rows, :] = (hg * u * s * (1.0 + g * (1.0 - s))).astype(jnp.bfloat16)
                cat[GUB + f, rows, :] = (hg * gs).astype(jnp.bfloat16)
            return 0

        lax.fori_loop(0, 6, body, 0)

    def partial(h, t):
        cat = cats[h]
        lhs = jnp.concatenate([cat[GGB + k] for k in range(12)], axis=1)
        rhs = jnp.concatenate([wg[t], wu[t]], axis=1)
        v = lax.dot_general(lhs, rhs, NT, preferred_element_type=jnp.float32)
        ps[h][t] = v.astype(jnp.bfloat16)

    def partial_y(h):
        def body(i, _):
            partial(h, mod4(cx + 2 - i) * 4 + mod4(cy + 2))
            return 0

        lax.fori_loop(0, 4, body, 0)

    def partial_x(h):
        def body(i, _):
            partial(h, mod4(cx + 2) * 4 + mod4(cy + 1 - i))
            return 0

        lax.fori_loop(0, 3, body, 0)

    def partial_rest(h):
        def body(i, _):
            partial(h, mod4(cx + 1 - lax.rem(i, 3)) * 4 + mod4(cy + 1 - i // 3))
            return 0

        lax.fori_loop(0, 9, body, 0)

    def rs(h, p):
        fx = p == 1
        c1, c2 = (cx, cy) if fx else (cy, cx)
        buf = ps[h]
        r0 = p * 128
        full, low, up = pl.ds(r0, 128), pl.ds(r0, 64), pl.ds(r0 + 64, 64)

        def dev(d1, d2):
            return (dp, tensor_at(fx, mod4(c1 + d1), mod4(c2 + d2)))

        def blk(d1, d2):
            return tensor_at(fx, mod4(c1 + d1), mod4(c2 + d2))

        def put(idx, d1, d2, rows, dst, e1, e2):
            send(buf.at[blk(d1, d2), rows, :], dst, rs_s.at[h, p, idx], rs_r.at[h, p, idx], dev(e1, e2))

        def got(idx, dst):
            rcopy(dst, dst, rs_s.at[h, p, idx], rs_r.at[h, p, idx], dev(1, 0)).wait_recv()

        def add(d1, d2, rows, *terms):
            b = blk(d1, d2)
            v = buf[b, rows, :].astype(jnp.float32)
            for ref in terms:
                v = v + ref[...].astype(jnp.float32)
            return b, v

        def addto(d1, d2, rows, *terms):
            b, v = add(d1, d2, rows, *terms)
            buf[b, rows, :] = v.astype(jnp.bfloat16)

        R1 = [[r1.at[h, p, j, k] for k in range(2)] for j in range(4)]
        R2 = [[r2.at[h, p, j, k] for k in range(2)] for j in range(4)]
        R3 = [r3.at[h, p, k] for k in range(2)]
        R4 = [r4.at[h, p, k] for k in range(2)]

        def s1(j):
            put(4 * j, 2, OFF2[j], low, R1[j][0], 1, 0)
            put(4 * j + 1, 2, OFF2[j], up, R1[j][1], -1, 0)

        def t1(j):
            got(4 * j, R1[j][0])
            addto(1, OFF2[j], low, R1[j][0])
            put(4 * j + 2, 1, OFF2[j], full, R2[j][0], 1, 0)
            got(4 * j + 1, R1[j][1])
            addto(-1, OFF2[j], up, R1[j][1])
            put(4 * j + 3, -1, OFF2[j], full, R2[j][1], -1, 0)

        def t2(j):
            got(4 * j + 2, R2[j][0])
            got(4 * j + 3, R2[j][1])
            addto(0, OFF2[j], full, R2[j][0], R2[j][1])
            if j == 0:
                put(16, 0, 2, low, R3[0], 0, 1)
                put(17, 0, 2, up, R3[1], 0, -1)

        def t3():
            got(16, R3[0])
            addto(0, 1, low, R3[0])
            put(18, 0, 1, full, R4[0], 0, 1)
            got(17, R3[1])
            addto(0, -1, up, R3[1])
            put(19, 0, -1, full, R4[1], 0, -1)

        def t4():
            got(18, R4[0])
            got(19, R4[1])
            _, v = add(0, 0, full, R4[0], R4[1])
            out_x[pl.ds(h * ROWS + r0, 128), :] = v.astype(jnp.bfloat16)

        return s1, t1, t2, t3, t4

    RS = [[rs(h, p) for p in range(2)] for h in range(2)]

    def rs_step(h, k, *a):
        for p in range(2):
            RS[h][p][k](*a)

    UN = 4

    def tiles_of(h):
        cat = cats[h]

        def body(q, carry):
            sq = list(carry)
            for i in range(UN):
                s = q * UN + i
                f, m, kd = sf[s], sm[s], sk[s]
                live = jnp.where(s < lc[0], 1.0, 0.0).astype(jnp.float32)
                li = jnp.where(kd == 2, HB + f, XB + m)
                ri = jnp.where(kd == 0, GGB + f, jnp.where(kd == 1, GUB + f, GB + m))
                for e in range(2):
                    rows = pl.ds(e * LEN, LEN)
                    v = lax.dot_general(
                        cat[li, rows, :], cat[ri, rows, :], TN, preferred_element_type=jnp.float32
                    )
                    v = v * live
                    tiles[2 * h + e, s] = v
                    sq[e] = sq[e] + jnp.sum((v * v).reshape(16, 8, TILE), axis=0)
            return tuple(sq)

        z = jnp.zeros((8, TILE), jnp.float32)
        sq = lax.fori_loop(0, SLOTS // UN, body, (z, z))
        for e in range(2):
            nr[me, pl.ds(2 * h + e, 1), :] = jnp.sum(sq[e], axis=0, keepdims=True)

    def norm_send():
        for k in range(1, 16):
            send(nr.at[me], nr.at[me], nr_s.at[k], nr_r.at[k], (dp, lax.rem(me + k, 16)))

    def norm_wait():
        for k in range(1, 16):
            src = nr.at[lax.rem(me + 16 - k, 16)]
            rcopy(src, src, nr_s.at[k], nr_r.at[k], (dp, lax.rem(me + k, 16))).wait_recv()
        tot = nr[0]
        for k in range(1, 16):
            tot = tot + nr[k]
        tot = jnp.sum(tot, axis=1, keepdims=True)
        clip = jnp.minimum(1.0, BOUND / jnp.sqrt(tot + 1e-06))
        return jnp.broadcast_to(clip, (8, TILE))

    def scaled(clip, g):
        cl = [clip[e : e + 1, :] for e in range(4)]

        def body(i, _):
            s = g * DPS + i
            v = cl[0] * tiles[0, s]
            for e in range(1, 4):
                v = v + cl[e] * tiles[e, s]
            v = v.astype(jnp.bfloat16)
            for z in range(4):
                for c in range(2):
                    ssum[z, c, s] = v[(2 * z + c) * 16 : (2 * z + c + 1) * 16, :]
            return 0

        lax.fori_loop(0, DPS, body, 0)
        sl = pl.ds(g * DPS, DPS)
        send(
            ssum.at[:, 1 - cc, sl], cr.at[:, sl], c_s.at[g], c_r.at[g], (cz * 2 + 1 - cc, me)
        )

    def core_sum(g):
        sl = pl.ds(g * DPS, DPS)
        rcopy(cr.at[:, sl], cr.at[:, sl], c_s.at[g], c_r.at[g], (cz * 2 + 1 - cc, me)).wait_recv()

        for k in range(1, 4):
            z = mod4(cz + k)
            v = ssum[z, cc, sl].astype(jnp.float32) + cr[z, sl].astype(jnp.float32)
            zs[k - 1, sl] = v.astype(jnp.bfloat16)
            send(zs.at[k - 1, sl], zr.at[k - 1, sl], z_s.at[k - 1, g], z_r.at[k - 1, g], (z * 2 + cc, me))

    def z_sum(g):
        sl = pl.ds(g * DPS, DPS)
        v = ssum[cz, cc, sl].astype(jnp.float32) + cr[cz, sl].astype(jnp.float32)
        for k in range(3):
            r = zr.at[k, sl]
            rcopy(r, r, z_s.at[k, g], z_r.at[k, g], (mod4(cz + k + 1) * 2 + cc, me)).wait_recv()
            v = v + zr[k, sl].astype(jnp.float32)
        out_b[sl] = v

    for c in own[:4]:
        c.wait()
    ag_step(0, 0)
    for c in own[4:]:
        c.wait()
    nr[me] = jnp.zeros((8, TILE), jnp.float32)
    ag_step(0, 1)
    ag_step(0, 2)
    ag_step(0, 3)
    for c in wcopies:
        c.wait()
    fwd(0, 0)
    ag_step(0, 4, 0)
    ag_step(0, 4, 1)
    ag_step(1, 0)
    ag_step(0, 4, 2)
    ag_step(0, 4, 3)
    fwd(0, -1)
    fwd(0, 1)
    ag_step(1, 1)
    ag_step(1, 2)
    for j in range(4):
        ag_step(0, 5, j)
    fwd(0, 2)
    ag_step(1, 3)
    pointwise(0)
    ag_step(1, 4, 0)
    fwd(1, 0)
    partial_y(0)
    ag_step(1, 4, 1)
    partial_x(0)
    partial_rest(0)
    ag_step(1, 4, 2)
    tiles_of(0)
    ag_step(1, 4, 3)
    for j in range(4):
        rs_step(0, 0, j)
    fwd(1, -1)
    fwd(1, 1)
    for j in range(4):
        rs_step(0, 1, j)
    for j in range(4):
        ag_step(1, 5, j)
    fwd(1, 2)
    pointwise(1)
    for j in range(4):
        rs_step(0, 2, j)
    partial_y(1)
    for j in range(4):
        RS[1][0][0](j)
    partial_x(1)
    for j in range(4):
        RS[1][1][0](j)
    rs_step(0, 3)
    tiles_of(1)
    norm_send()
    partial_rest(1)
    for j in range(4):
        rs_step(1, 1, j)
    clip = norm_wait()
    for g in range(DPG):
        scaled(clip, g)
    rs_step(0, 4)
    core_sum(0)
    for j in range(2):
        rs_step(1, 2, j)
    core_sum(1)
    for j in range(2, 4):
        rs_step(1, 2, j)
    core_sum(2)
    rs_step(1, 3)
    rs_step(1, 4)
    for g in range(DPG):
        z_sum(g)
    for c in sends:
        c.wait_send()


def per_device(
    tokens,
    out_grad,
    gate_weight,
    up_weight,
    down_weight,
    slot_ffn_block,
    slot_model_block,
    slot_kind,
    live_count,
):
    bf, f32 = jnp.bfloat16, jnp.float32
    anyspec = pl.BlockSpec(memory_space=pl.ANY)
    smem = pl.BlockSpec(memory_space=pltpu.SMEM)
    vmem = pl.BlockSpec(memory_space=pltpu.VMEM)
    dma = pltpu.SemaphoreType.DMA
    return pl.pallas_call(
        kernel,
        out_shape=(
            jax.ShapeDtypeStruct((512, 256), bf),
            jax.ShapeDtypeStruct((SLOTS, 16, TILE), f32),
        ),
        in_specs=[anyspec] * 5 + [smem] * 4,
        out_specs=(vmem, vmem),
        scratch_shapes=[
            pltpu.VMEM((BLOCKS, ROWS, TILE), bf),
            pltpu.VMEM((BLOCKS, ROWS, TILE), bf),
            pltpu.VMEM((16, 256, 768), bf),
            pltpu.VMEM((16, 256, 768), bf),
            pltpu.VMEM((4, 768, 1024), bf),
            pltpu.VMEM((6, ROWS, TILE), f32),
            pltpu.VMEM((6, ROWS, TILE), f32),
            pltpu.VMEM((6, ROWS, TILE), f32),
            pltpu.VMEM((16, ROWS, 256), bf),
            pltpu.VMEM((16, ROWS, 256), bf),
            pltpu.VMEM((2, 2, 4, 2, 64, 256), bf),
            pltpu.VMEM((2, 2, 4, 2, 128, 256), bf),
            pltpu.VMEM((2, 2, 2, 64, 256), bf),
            pltpu.VMEM((2, 2, 2, 128, 256), bf),
            pltpu.VMEM((4, SLOTS, TILE, TILE), f32),
            pltpu.VMEM((16, 8, TILE), f32),
            pltpu.VMEM((4, 2, SLOTS, 16, TILE), bf),
            pltpu.VMEM((4, SLOTS, 16, TILE), bf),
            pltpu.VMEM((3, SLOTS, 16, TILE), bf),
            pltpu.VMEM((3, SLOTS, 16, TILE), bf),
            dma((2, 2, 2)),
            dma((6,)),
            dma((2, 2, 20)),
            dma((2, 2, 20)),
            dma((2, 2, 20)),
            dma((2, 2, 20)),
            dma((16,)),
            dma((16,)),
            dma((DPG,)),
            dma((DPG,)),
            dma((3, DPG)),
            dma((3, DPG)),
        ],
        compiler_params=pltpu.CompilerParams(
            collective_id=0, has_side_effects=True, vmem_limit_bytes=62 << 20
        ),
        cost_estimate=pl.CostEstimate(
            flops=17_000_000_000, bytes_accessed=20_000_000, transcendentals=400_000
        ),
    )(
        tokens,
        out_grad,
        gate_weight.reshape(16, 256, 768),
        up_weight.reshape(16, 256, 768),
        down_weight,
        slot_ffn_block,
        slot_model_block,
        slot_kind,
        live_count,
    )


def solution(mesh):
    return jax.shard_map(
        per_device,
        mesh=mesh,
        in_specs=(
            P("dp", "tensor"),
            P("dp", "tensor"),
            P(None, "tensor"),
            P(None, "tensor"),
            P("tensor", None),
            P("tensor"),
            P("tensor"),
            P("tensor"),
            P("tensor"),
        ),
        out_specs=(P("dp", "tensor"), P("tensor", "dp", None)),
        check_vma=False,
    )
```

```python
import math

import jax
import jax.numpy as jnp
from jax import lax
from jax.experimental import pallas as pl
from jax.experimental.pallas import tpu as pltpu
from jax.sharding import PartitionSpec as P

TILE = 128
LEN = 128
CHUNKS = (256, 256)
STARTS = tuple(sum(CHUNKS[:i]) for i in range(len(CHUNKS)))
NC = len(CHUNKS)
SEQ0 = tuple(v // LEN for v in STARTS)
NSEQ = tuple(v // LEN for v in CHUNKS)
SLOTS = 48
NX = 4
XB, GB, HB, GGB, GUB = 0, 32, 64, 70, 76
BLOCKS = 82
OFF = (0, -1, 1, 2)
OFF2 = (2, 1, -1, 0)
MESH = pl.DeviceIdType.MESH
BOUND = 0.33 * TILE * math.sqrt(LEN * 768)
NT = (((1,), (1,)), ((), ()))
TN = (((0,), (0,)), ((), ()))
NT1 = 1 + NSEQ[-1]


def mod4(v):
    return lax.rem(v + 8, 4)


def kernel(
    tok,
    og,
    gw,
    uw,
    dw,
    sf,
    sm,
    sk,
    lc,
    out_x,
    out_b,
    cats,
    wg,
    wu,
    wd,
    acc_g,
    acc_u,
    acc_h,
    ps,
    r1,
    r2,
    r3,
    r4,
    tiles,
    nr,
    xs,
    xr,
    cs,
    cr,
    zs,
    zr,
    own_sem,
    w_sem,
    ag_s,
    ag_r,
    rs_s,
    rs_r,
    nr_s,
    nr_r,
    x_s,
    x_r,
    c_s,
    c_r,
    z_s,
    z_r,
    o_sem,
    ox,
    ob,
):
    dp = lax.axis_index("dp")
    me = lax.axis_index("tensor")
    cx, cy = me // 4, lax.rem(me, 4)
    cz, cc = dp // 2, lax.rem(dp, 2)
    sends = []

    own = []
    for h in range(NC):
        for arr, src in ((0, tok), (1, og)):
            for k in range(2):
                c = pltpu.make_async_copy(
                    src.at[pl.ds(STARTS[h], CHUNKS[h]), pl.ds(k * TILE, TILE)],
                    cats[h].at[32 * arr + 2 * me + k],
                    own_sem.at[h, arr, k],
                )
                c.start()
                own.append(c)
    wcopies = [
        pltpu.make_async_copy(gw, wg, w_sem.at[0]),
        pltpu.make_async_copy(uw, wu, w_sem.at[1]),
    ] + [
        pltpu.make_async_copy(dw.at[:, pl.ds(1024 * i, 1024)], wd.at[i], w_sem.at[2 + i])
        for i in range(4)
    ]
    for c in wcopies:
        c.start()

    barrier = pltpu.get_barrier_semaphore()
    z_next = [(mod4(cz + d) * 2 + cc, me) for d in (1, -1)]
    near = [
        (dp, mod4(cx + 1) * 4 + cy),
        (dp, mod4(cx - 1) * 4 + cy),
        (dp, cx * 4 + mod4(cy + 1)),
        (dp, cx * 4 + mod4(cy - 1)),
        (cz * 2 + 1 - cc, me),
    ] + z_next
    for dev in near:
        pl.semaphore_signal(barrier, inc=1, device_id=dev, device_id_type=MESH)
    pl.semaphore_wait(barrier, len(near))

    def rcopy(src, dst, ssem, rsem, dev):
        return pltpu.make_async_remote_copy(
            src_ref=src, dst_ref=dst, send_sem=ssem, recv_sem=rsem, device_id=dev, device_id_type=MESH
        )

    def send(src, dst, ssem, rsem, dev):
        c = rcopy(src, dst, ssem, rsem, dev)
        c.start()
        sends.append(c)

    outs = []

    def put_out(src, dst, idx):
        c = pltpu.make_async_copy(src, dst, o_sem.at[idx])
        c.start()
        outs.append(c)

    def tensor_at(first_is_x, a1, a2):
        return a1 * 4 + a2 if first_is_x else a2 * 4 + a1

    def ag(h, arr):
        R = CHUNKS[h]
        fx = arr == 0
        c1, c2 = (cx, cy) if fx else (cy, cx)

        def dev(d1, d2):
            return (dp, tensor_at(fx, mod4(c1 + d1), mod4(c2 + d2)))

        def region(d1, d2, part):
            t = tensor_at(fx, mod4(c1 + d1), mod4(c2 + d2))
            rows = (pl.ds(0, R), pl.ds(0, R // 2), pl.ds(R // 2, R // 2))[part]
            return cats[h].at[pl.ds(32 * arr + 2 * t, 2), rows, :]

        def put(idx, d1, d2, part, e1, e2):
            r = region(d1, d2, part)
            send(r, r, ag_s.at[h, arr, idx], ag_r.at[h, arr, idx], dev(e1, e2))

        def got(idx, d1, d2, part):
            r = region(d1, d2, part)
            rcopy(r, r, ag_s.at[h, arr, idx], ag_r.at[h, arr, idx], dev(1, 0)).wait_recv()

        def start():
            put(0, 0, 0, 0, 1, 0)
            put(1, 0, 0, 0, -1, 0)
            put(4, 0, 0, 0, 0, 1)
            put(5, 0, 0, 0, 0, -1)

        def spread(j):
            put(4 + 4 * j, OFF[j], 0, 0, 0, 1)
            put(5 + 4 * j, OFF[j], 0, 0, 0, -1)

        def e1():
            got(0, -1, 0, 0)
            put(2, -1, 0, 1, 1, 0)
            spread(1)

        def e2():
            got(1, 1, 0, 0)
            put(3, 1, 0, 2, -1, 0)
            spread(2)

        def e3():
            got(2, 2, 0, 1)
            got(3, 2, 0, 2)
            spread(3)

        def e4(j):
            got(4 + 4 * j, OFF[j], -1, 0)
            put(6 + 4 * j, OFF[j], -1, 1, 0, 1)
            got(5 + 4 * j, OFF[j], 1, 0)
            put(7 + 4 * j, OFF[j], 1, 2, 0, -1)

        def e5(j):
            got(6 + 4 * j, OFF[j], 2, 1)
            got(7 + 4 * j, OFF[j], 2, 2)

        return start, e1, e2, e3, e4, e5

    AG = [[ag(h, arr) for arr in range(2)] for h in range(NC)]

    def ag_step(h, k, *a):
        for arr in range(2):
            AG[h][arr][k](*a)

    def fwd(h, off, n):
        cat, rr = cats[h], pl.ds(0, CHUNKS[h])
        yy, xx = mod4(cy + off), mod4(cx + off)
        cols = pl.ds(n * 256, 256)

        def total(acc, v):
            for k in range(2):
                vk = v[:, k * TILE : (k + 1) * TILE]
                acc[2 * n + k, rr, :] = vk if off == 0 else acc[2 * n + k, rr, :] + vk

        lhs = jnp.concatenate(
            [cat[2 * (4 * i + yy) + k] for i in range(4) for k in range(2)], axis=1
        )
        for w, acc in ((wg, acc_g), (wu, acc_u)):
            rhs = jnp.concatenate([w[4 * i + yy, :, cols] for i in range(4)], axis=0)
            total(acc, jnp.dot(lhs, rhs, preferred_element_type=jnp.float32))
        lhs = jnp.concatenate([cat[GB + 8 * xx + k] for k in range(8)], axis=1)
        total(acc_h, lax.dot_general(lhs, wd[xx, cols, :], NT, preferred_element_type=jnp.float32))

    def pointwise(h):
        cat = cats[h]

        def body(f, _):
            for r in range(CHUNKS[h] // 64):
                rows = pl.ds(r * 64, 64)
                g, u, hg = acc_g[f, rows, :], acc_u[f, rows, :], acc_h[f, rows, :]
                s = 1.0 / (1.0 + jnp.exp(-g))
                gs = g * s
                cat[HB + f, rows, :] = (gs * u).astype(jnp.bfloat16)
                cat[GGB + f, rows, :] = (hg * u * s * (1.0 + g * (1.0 - s))).astype(jnp.bfloat16)
                cat[GUB + f, rows, :] = (hg * gs).astype(jnp.bfloat16)
            return 0

        lax.fori_loop(0, 6, body, 0)

    def partial(h, off, half):
        cat = cats[h]
        yy = mod4(cy + off)
        at = [4 * i + yy for i in (2 * half, 2 * half + 1)]
        lhs = jnp.concatenate(
            [jnp.concatenate([wg[t], wu[t]], axis=1) for t in at], axis=0
        )
        rhs = jnp.concatenate([cat[GGB + k] for k in range(12)], axis=1)
        v = lax.dot_general(lhs, rhs, NT, preferred_element_type=jnp.float32)
        v = v.astype(jnp.bfloat16)
        for i, t in enumerate(at):
            ps[h][t] = v[256 * i : 256 * (i + 1)]

    def rs(h, p):
        fx = p == 1
        c1, c2 = (cx, cy) if fx else (cy, cx)
        buf = ps[h]
        r0 = p * 128
        full, low, up = pl.ds(r0, 128), pl.ds(r0, 64), pl.ds(r0 + 64, 64)

        def dev(d1, d2):
            return (dp, tensor_at(fx, mod4(c1 + d1), mod4(c2 + d2)))

        def blk(d1, d2):
            return tensor_at(fx, mod4(c1 + d1), mod4(c2 + d2))

        def put(idx, d1, d2, rows, dst, e1, e2):
            send(buf.at[blk(d1, d2), rows, :], dst, rs_s.at[h, p, idx], rs_r.at[h, p, idx], dev(e1, e2))

        def got(idx, dst):
            rcopy(dst, dst, rs_s.at[h, p, idx], rs_r.at[h, p, idx], dev(1, 0)).wait_recv()

        def add(d1, d2, rows, *terms):
            b = blk(d1, d2)
            v = buf[b, rows, :].astype(jnp.float32)
            for ref in terms:
                v = v + ref[...].astype(jnp.float32)
            return b, v

        def addto(d1, d2, rows, *terms):
            b, v = add(d1, d2, rows, *terms)
            buf[b, rows, :] = v.astype(jnp.bfloat16)

        R1 = [[r1[h].at[p, j, k] for k in range(2)] for j in range(4)]
        R2 = [[r2[h].at[p, j, k] for k in range(2)] for j in range(4)]
        R3 = [r3[h].at[p, k] for k in range(2)]
        R4 = [r4[h].at[p, k] for k in range(2)]

        def s1(j):
            put(4 * j, 2, OFF2[j], low, R1[j][0], 1, 0)
            put(4 * j + 1, 2, OFF2[j], up, R1[j][1], -1, 0)

        def t1(j):
            got(4 * j, R1[j][0])
            addto(1, OFF2[j], low, R1[j][0])
            put(4 * j + 2, 1, OFF2[j], full, R2[j][0], 1, 0)
            got(4 * j + 1, R1[j][1])
            addto(-1, OFF2[j], up, R1[j][1])
            put(4 * j + 3, -1, OFF2[j], full, R2[j][1], -1, 0)

        def t2(j):
            got(4 * j + 2, R2[j][0])
            got(4 * j + 3, R2[j][1])
            addto(0, OFF2[j], full, R2[j][0], R2[j][1])
            if j == 0:
                put(16, 0, 2, low, R3[0], 0, 1)
                put(17, 0, 2, up, R3[1], 0, -1)

        def t3():
            got(16, R3[0])
            addto(0, 1, low, R3[0])
            put(18, 0, 1, full, R4[0], 0, 1)
            got(17, R3[1])
            addto(0, -1, up, R3[1])
            put(19, 0, -1, full, R4[1], 0, -1)

        def t4():
            got(18, R4[0])
            got(19, R4[1])
            _, v = add(0, 0, full, R4[0], R4[1])
            rows, cols = pl.ds(STARTS[h], CHUNKS[h]), pl.ds(r0, 128)
            ox[rows, cols] = v.T.astype(jnp.bfloat16)
            put_out(ox.at[rows, cols], out_x.at[rows, cols], 2 * h + p)

        return s1, t1, t2, t3, t4

    RS = [[rs(h, p) for p in range(2)] for h in range(NC)]

    def rs_step(h, k, *a):
        for p in range(2):
            RS[h][p][k](*a)

    UN = 4

    squares = {}

    def tiles_of(h, q0, q1):
        cat, ne = cats[h], NSEQ[h]

        def body(q, carry):
            sq = list(carry)
            for i in range(UN):
                s = q * UN + i
                f, m, kd = sf[s], sm[s], sk[s]
                live = jnp.where(s < lc[0], 1.0, 0.0).astype(jnp.float32)
                li = jnp.where(kd == 2, HB + f, XB + m)
                ri = jnp.where(kd == 0, GGB + f, jnp.where(kd == 1, GUB + f, GB + m))
                for e in range(ne):
                    rows = pl.ds(e * LEN, LEN)
                    v = lax.dot_general(
                        cat[li, rows, :], cat[ri, rows, :], TN, preferred_element_type=jnp.float32
                    )
                    v = v * live
                    tiles[SEQ0[h] + e, s] = v
                    sq[e] = sq[e] + jnp.sum((v * v).reshape(16, 8, TILE), axis=0)
            return tuple(sq)

        z = jnp.zeros((8, TILE), jnp.float32)
        sq = lax.fori_loop(q0, q1, body, squares.pop(h, (z,) * ne))
        if q1 < SLOTS // UN:
            squares[h] = sq
            return
        for e in range(ne):
            nr[h, me, pl.ds(e, 1), :] = jnp.sum(sq[e], axis=0, keepdims=True)

    def norm_send(h):
        for k in range(1, 16):
            r = nr.at[h, me]
            send(r, r, nr_s.at[h, k], nr_r.at[h, k], (dp, lax.rem(me + k, 16)))

    def norm_wait(h):
        for k in range(1, 16):
            src = nr.at[h, lax.rem(me + 16 - k, 16)]
            rcopy(src, src, nr_s.at[h, k], nr_r.at[h, k], (dp, lax.rem(me + k, 16))).wait_recv()
        tot = nr[h, 0]
        for k in range(1, 16):
            tot = tot + nr[h, k]
        tot = jnp.sum(tot, axis=1, keepdims=True)
        clip = jnp.minimum(1.0, BOUND / jnp.sqrt(tot + 1e-06))
        clip = jnp.broadcast_to(clip, (8, TILE))
        return [clip[e : e + 1, :] for e in range(NSEQ[h])]

    def fold(cl):
        def body(s, _):
            v = cl[0] * tiles[0, s]
            for e in range(1, len(cl)):
                v = v + cl[e] * tiles[e, s]
            tiles[0, s] = v
            return 0

        lax.fori_loop(0, SLOTS, body, 0)

    partner = (cz * 2 + 1 - cc, me)
    terms = [0] + [SEQ0[-1] + e for e in range(NSEQ[-1])]

    def rows_of(z, c):
        return pl.ds(pl.multiple_of((2 * z + c) * 16, 16), 16)

    def to_partner(k):
        def body(s, _):
            for z in range(4):
                xs[k, z, s] = tiles[terms[k], s, rows_of(z, 1 - cc), :].astype(jnp.bfloat16)
            return 0

        lax.fori_loop(0, SLOTS, body, 0)
        send(xs.at[k], xr.at[k], x_s.at[k], x_r.at[k], partner)

    def clip_to_partner(cl):
        for e in range(NSEQ[-1]):
            cs[pl.ds(e, 1), :] = cl[e]
        send(cs, cr, c_s.at[0], c_r.at[0], partner)

    def partner_clip():
        rcopy(cr, cr, c_s.at[0], c_r.at[0], partner).wait_recv()
        return [cr[pl.ds(e, 1), :] for e in range(NSEQ[-1])]

    def from_partner(k):
        rcopy(xr.at[k], xr.at[k], x_s.at[k], x_r.at[k], partner).wait_recv()

    def combined(z, s, cl, pcl):
        v = tiles[0, s, rows_of(z, cc), :] + xr[0, z, s].astype(jnp.float32)
        for e in range(NSEQ[-1]):
            v = v + cl[e] * tiles[terms[e + 1], s, rows_of(z, cc), :]
            v = v + pcl[e] * xr[e + 1, z, s].astype(jnp.float32)
        return v

    HALF = (pl.ds(0, SLOTS // 2), pl.ds(SLOTS // 2, SLOTS // 2))

    def combine(d, half, cl, pcl):
        z = mod4(cz + d)

        def body(i, _):
            s = half * (SLOTS // 2) + i
            zs[z, s] = combined(z, s, cl, pcl).astype(jnp.bfloat16)
            return 0

        lax.fori_loop(0, SLOTS // 2, body, 0)

    def zput(idx, d_block, half, dst, d):
        send(
            zs.at[mod4(cz + d_block), HALF[half]],
            zr.at[dst, HALF[half]],
            z_s.at[idx],
            z_r.at[idx],
            (mod4(cz + d) * 2 + cc, me),
        )

    def zgot(idx, dst, half):
        r = zr.at[dst, HALF[half]]
        rcopy(r, r, z_s.at[idx], z_r.at[idx], (mod4(cz + 1) * 2 + cc, me)).wait_recv()

    def zadd(d_block, half, src):
        z = mod4(cz + d_block)
        v = zs[z, HALF[half]].astype(jnp.float32) + zr[src, HALF[half]].astype(jnp.float32)
        zs[z, HALF[half]] = v.astype(jnp.bfloat16)

    def z_start(cl, pcl):
        combine(2, 0, cl, pcl)
        zput(0, 2, 0, 0, 1)
        combine(2, 1, cl, pcl)
        zput(1, 2, 1, 1, -1)
        combine(1, 1, cl, pcl)
        zput(2, 1, 1, 2, 1)
        combine(-1, 0, cl, pcl)
        zput(3, -1, 0, 3, -1)
        combine(1, 0, cl, pcl)
        combine(-1, 1, cl, pcl)

    def z_pass():
        zgot(0, 0, 0)
        zadd(1, 0, 0)
        zput(4, 1, 0, 2, 1)
        zgot(1, 1, 1)
        zadd(-1, 1, 1)
        zput(5, -1, 1, 3, -1)

    def z_own(cl, pcl):
        def body(s, _):
            ob[s] = combined(cz, s, cl, pcl)
            return 0

        lax.fori_loop(0, SLOTS, body, 0)

    def z_end(half):
        zgot(2 if half else 4, 2, half)
        zgot(5 if half else 3, 3, half)
        sl = HALF[half]
        ob[sl] = ob[sl] + zr[2, sl].astype(jnp.float32) + zr[3, sl].astype(jnp.float32)
        put_out(ob.at[sl], out_b.at[sl], 2 * NC + half)

    J = range(4)
    N = range(3)
    for c in own[:4]:
        c.wait()
    ag_step(0, 0)
    for c in own[4:]:
        c.wait()
    nr[:, me] = jnp.zeros((NC, 8, TILE), jnp.float32)
    cs[...] = jnp.zeros((8, TILE), jnp.float32)
    ag_step(0, 1)
    ag_step(0, 2)
    ag_step(1, 0)
    ag_step(0, 3)
    for c in wcopies:
        c.wait()
    ag_step(0, 4, 0)
    for n in N:
        fwd(0, 0, n)
        ag_step(0, 4, n + 1)
    ag_step(1, 1)
    fwd(0, -1, 0)
    ag_step(1, 2)
    fwd(0, -1, 1)
    ag_step(0, 5, 0)
    fwd(0, -1, 2)
    ag_step(1, 3)
    for n in N:
        fwd(0, 1, n)
        ag_step(0, 5, n + 1)
    for n in N:
        fwd(0, 2, n)
    ag_step(1, 4, 0)
    pointwise(0)
    for k in J:
        partial(0, OFF2[k], 0)
        partial(0, OFF2[k], 1)
        if k == 1:
            ag_step(1, 4, 1)
    tiles_of(0, 0, 6)
    ag_step(1, 4, 2)
    tiles_of(0, 6, 12)
    norm_send(0)
    ag_step(1, 4, 3)
    for k in J:
        rs_step(0, 0, k)
    for n in N:
        fwd(1, 0, n)
    for n in N:
        fwd(1, -1, n)
    for j in J:
        rs_step(0, 1, j)
    for n in N:
        fwd(1, 1, n)
    for j in J:
        ag_step(1, 5, j)
    for n in N:
        fwd(1, 2, n)
    pointwise(1)
    tiles_of(1, 0, 6)
    rs_step(0, 2, 0)
    rs_step(0, 2, 1)
    tiles_of(1, 6, 12)
    norm_send(1)
    for k in range(1, NT1):
        to_partner(k)
    rs_step(0, 2, 2)
    rs_step(0, 2, 3)
    rs_step(0, 3)
    fold(norm_wait(0))
    to_partner(0)
    partial(1, 2, 0)
    partial(1, 2, 1)
    for k in J:
        RS[1][0][0](k)
    RS[1][1][0](0)
    partial(1, 1, 0)
    partial(1, 1, 1)
    RS[1][1][0](1)
    clip = norm_wait(1)
    clip_to_partner(clip)
    for k in (2, 3):
        partial(1, OFF2[k], 0)
        partial(1, OFF2[k], 1)
        RS[1][1][0](k)
    for k in range(NT1):
        from_partner(k)
    pclip = partner_clip()
    z_start(clip, pclip)
    for j in J:
        rs_step(1, 1, j)
    rs_step(0, 4)
    z_pass()
    z_own(clip, pclip)
    for j in J:
        rs_step(1, 2, j)
    rs_step(1, 3)
    z_end(1)
    z_end(0)
    rs_step(1, 4)
    for c in sends:
        c.wait_send()
    for c in outs:
        c.wait()


def hand_out(x, b, out_x, out_b, vx, vb, sem):
    ins = [pltpu.make_async_copy(x, vx, sem.at[0]), pltpu.make_async_copy(b, vb, sem.at[1])]
    outs = [pltpu.make_async_copy(vx, out_x, sem.at[2]), pltpu.make_async_copy(vb, out_b, sem.at[3])]
    for c in ins:
        c.start()
    for i, o in zip(ins, outs):
        i.wait()
        o.start()
    for o in outs:
        o.wait()


def per_device(
    tokens,
    out_grad,
    gate_weight,
    up_weight,
    down_weight,
    slot_ffn_block,
    slot_model_block,
    slot_kind,
    live_count,
):
    bf, f32 = jnp.bfloat16, jnp.float32
    anyspec = pl.BlockSpec(memory_space=pl.ANY)
    smem = pl.BlockSpec(memory_space=pltpu.SMEM)
    dma = pltpu.SemaphoreType.DMA
    grad_x, grad_b = pl.pallas_call(
        kernel,
        out_shape=(
            jax.ShapeDtypeStruct((512, 256), bf),
            jax.ShapeDtypeStruct((SLOTS, 16, TILE), f32),
        ),
        in_specs=[anyspec] * 5 + [smem] * 4,
        out_specs=(anyspec, anyspec),
        scratch_shapes=[
            [pltpu.VMEM((BLOCKS, r, TILE), bf) for r in CHUNKS],
            pltpu.VMEM((16, 256, 768), bf),
            pltpu.VMEM((16, 256, 768), bf),
            pltpu.VMEM((4, 768, 1024), bf),
            pltpu.VMEM((6, max(CHUNKS), TILE), f32),
            pltpu.VMEM((6, max(CHUNKS), TILE), f32),
            pltpu.VMEM((6, max(CHUNKS), TILE), f32),
            [pltpu.VMEM((16, 256, r), bf) for r in CHUNKS],
            [pltpu.VMEM((2, 4, 2, 64, r), bf) for r in CHUNKS],
            [pltpu.VMEM((2, 4, 2, 128, r), bf) for r in CHUNKS],
            [pltpu.VMEM((2, 2, 64, r), bf) for r in CHUNKS],
            [pltpu.VMEM((2, 2, 128, r), bf) for r in CHUNKS],
            pltpu.VMEM((4, SLOTS, TILE, TILE), f32),
            pltpu.VMEM((NC, 16, 8, TILE), f32),
            pltpu.VMEM((NT1, 4, SLOTS, 16, TILE), bf),
            pltpu.VMEM((NT1, 4, SLOTS, 16, TILE), bf),
            pltpu.VMEM((8, TILE), f32),
            pltpu.VMEM((8, TILE), f32),
            pltpu.VMEM((4, SLOTS, 16, TILE), bf),
            pltpu.VMEM((4, SLOTS, 16, TILE), bf),
            dma((NC, 2, 2)),
            dma((6,)),
            dma((NC, 2, 20)),
            dma((NC, 2, 20)),
            dma((NC, 2, 20)),
            dma((NC, 2, 20)),
            dma((NC, 16)),
            dma((NC, 16)),
            dma((NT1,)),
            dma((NT1,)),
            dma((1,)),
            dma((1,)),
            dma((6,)),
            dma((6,)),
            dma((2 * NC + 2,)),
            pltpu.VMEM((512, 256), bf),
            pltpu.VMEM((SLOTS, 16, TILE), f32),
        ],
        compiler_params=pltpu.CompilerParams(
            collective_id=0, has_side_effects=True, vmem_limit_bytes=62 << 20
        ),
        cost_estimate=pl.CostEstimate(
            flops=17_000_000_000, bytes_accessed=20_000_000, transcendentals=400_000
        ),
    )(
        tokens,
        out_grad,
        gate_weight.reshape(16, 256, 768),
        up_weight.reshape(16, 256, 768),
        down_weight,
        slot_ffn_block,
        slot_model_block,
        slot_kind,
        live_count,
    )
    return pl.pallas_call(
        hand_out,
        out_shape=(
            jax.ShapeDtypeStruct((512, 256), bf),
            jax.ShapeDtypeStruct((SLOTS, 16, TILE), f32),
        ),
        in_specs=[anyspec] * 2,
        out_specs=(anyspec, anyspec),
        scratch_shapes=[
            pltpu.VMEM((512, 256), bf),
            pltpu.VMEM((SLOTS, 16, TILE), f32),
            dma((4,)),
        ],
    )(grad_x, grad_b)


def solution(mesh):
    return jax.shard_map(
        per_device,
        mesh=mesh,
        in_specs=(
            P("dp", "tensor"),
            P("dp", "tensor"),
            P(None, "tensor"),
            P(None, "tensor"),
            P("tensor", None),
            P("tensor"),
            P("tensor"),
            P("tensor"),
            P("tensor"),
        ),
        out_specs=(P("dp", "tensor"), P("tensor", "dp", None)),
        check_vma=False,
    )
```

```python
import math

import jax
import jax.numpy as jnp
from jax import lax
from jax.experimental import pallas as pl
from jax.experimental.pallas import tpu as pltpu
from jax.sharding import PartitionSpec as P

TILE = 128
LEN = 128
CHUNKS = (256, 256)
STARTS = tuple(sum(CHUNKS[:i]) for i in range(len(CHUNKS)))
NC = len(CHUNKS)
SEQ0 = tuple(v // LEN for v in STARTS)
NSEQ = tuple(v // LEN for v in CHUNKS)
SLOTS = 48
NX = 4
XB, GB, HB, GGB, GUB = 0, 32, 64, 70, 76
BLOCKS = 82
OFF = (0, -1, 1, 2)
OFF2 = (2, 1, -1, 0)
MESH = pl.DeviceIdType.MESH
BOUND = 0.33 * TILE * math.sqrt(LEN * 768)
NT = (((1,), (1,)), ((), ()))
TN = (((0,), (0,)), ((), ()))
NT1 = 1 + NSEQ[-1]


def mod4(v):
    return lax.rem(v + 8, 4)


def kernel(
    tok,
    og,
    gw,
    uw,
    dw,
    sf,
    sm,
    sk,
    lc,
    out_x,
    out_b,
    cats,
    wg,
    wu,
    wd,
    acc_g,
    acc_u,
    acc_h,
    ps,
    r1,
    r2,
    r3,
    r4,
    tiles,
    nr,
    xs,
    xr,
    cs,
    cr,
    zs,
    zr,
    own_sem,
    w_sem,
    ag_s,
    ag_r,
    rs_s,
    rs_r,
    nr_s,
    nr_r,
    x_s,
    x_r,
    c_s,
    c_r,
    z_s,
    z_r,
    o_sem,
    ox,
    ob,
):
    dp = lax.axis_index("dp")
    me = lax.axis_index("tensor")
    cx, cy = me // 4, lax.rem(me, 4)
    cz, cc = dp // 2, lax.rem(dp, 2)
    sends = []

    own = []
    for h in range(NC):
        for arr, src in ((0, tok), (1, og)):
            for k in range(2):
                c = pltpu.make_async_copy(
                    src.at[pl.ds(STARTS[h], CHUNKS[h]), pl.ds(k * TILE, TILE)],
                    cats[h].at[32 * arr + 2 * me + k],
                    own_sem.at[h, arr, k],
                )
                c.start()
                own.append(c)
    wcopies = [
        pltpu.make_async_copy(gw, wg, w_sem.at[0]),
        pltpu.make_async_copy(uw, wu, w_sem.at[1]),
    ] + [
        pltpu.make_async_copy(dw.at[:, pl.ds(1024 * i, 1024)], wd.at[i], w_sem.at[2 + i])
        for i in range(4)
    ]
    for c in wcopies:
        c.start()

    barrier = pltpu.get_barrier_semaphore()
    z_next = [(mod4(cz + d) * 2 + cc, me) for d in (1, -1)]
    near = [
        (dp, mod4(cx + 1) * 4 + cy),
        (dp, mod4(cx - 1) * 4 + cy),
        (dp, cx * 4 + mod4(cy + 1)),
        (dp, cx * 4 + mod4(cy - 1)),
        (cz * 2 + 1 - cc, me),
    ] + z_next
    for dev in near:
        pl.semaphore_signal(barrier, inc=1, device_id=dev, device_id_type=MESH)
    pl.semaphore_wait(barrier, len(near))

    def rcopy(src, dst, ssem, rsem, dev):
        return pltpu.make_async_remote_copy(
            src_ref=src, dst_ref=dst, send_sem=ssem, recv_sem=rsem, device_id=dev, device_id_type=MESH
        )

    def send(src, dst, ssem, rsem, dev):
        c = rcopy(src, dst, ssem, rsem, dev)
        c.start()
        sends.append(c)

    outs = []

    def put_out(src, dst, idx):
        c = pltpu.make_async_copy(src, dst, o_sem.at[idx])
        c.start()
        outs.append(c)

    def tensor_at(first_is_x, a1, a2):
        return a1 * 4 + a2 if first_is_x else a2 * 4 + a1

    def ag(h, arr):
        R = CHUNKS[h]
        fx = arr == 0
        c1, c2 = (cx, cy) if fx else (cy, cx)

        def dev(d1, d2):
            return (dp, tensor_at(fx, mod4(c1 + d1), mod4(c2 + d2)))

        def region(d1, d2, part):
            t = tensor_at(fx, mod4(c1 + d1), mod4(c2 + d2))
            rows = (pl.ds(0, R), pl.ds(0, R // 2), pl.ds(R // 2, R // 2))[part]
            return cats[h].at[pl.ds(32 * arr + 2 * t, 2), rows, :]

        def put(idx, d1, d2, part, e1, e2):
            r = region(d1, d2, part)
            send(r, r, ag_s.at[h, arr, idx], ag_r.at[h, arr, idx], dev(e1, e2))

        def got(idx, d1, d2, part):
            r = region(d1, d2, part)
            rcopy(r, r, ag_s.at[h, arr, idx], ag_r.at[h, arr, idx], dev(1, 0)).wait_recv()

        def start():
            put(0, 0, 0, 0, 1, 0)
            put(1, 0, 0, 0, -1, 0)
            put(4, 0, 0, 0, 0, 1)
            put(5, 0, 0, 0, 0, -1)

        def spread(j):
            put(4 + 4 * j, OFF[j], 0, 0, 0, 1)
            put(5 + 4 * j, OFF[j], 0, 0, 0, -1)

        def e1():
            got(0, -1, 0, 0)
            put(2, -1, 0, 1, 1, 0)
            spread(1)

        def e2():
            got(1, 1, 0, 0)
            put(3, 1, 0, 2, -1, 0)
            spread(2)

        def e3():
            got(2, 2, 0, 1)
            got(3, 2, 0, 2)
            spread(3)

        def e4(j):
            got(4 + 4 * j, OFF[j], -1, 0)
            put(6 + 4 * j, OFF[j], -1, 1, 0, 1)
            got(5 + 4 * j, OFF[j], 1, 0)
            put(7 + 4 * j, OFF[j], 1, 2, 0, -1)

        def e5(j):
            got(6 + 4 * j, OFF[j], 2, 1)
            got(7 + 4 * j, OFF[j], 2, 2)

        return start, e1, e2, e3, e4, e5

    AG = [[ag(h, arr) for arr in range(2)] for h in range(NC)]

    def ag_step(h, k, *a):
        for arr in range(2):
            AG[h][arr][k](*a)

    def fwd(h, off, n):
        cat, rr = cats[h], pl.ds(0, CHUNKS[h])
        yy, xx = mod4(cy + off), mod4(cx + off)
        cols = pl.ds(n * 256, 256)

        def total(acc, v):
            for k in range(2):
                vk = v[:, k * TILE : (k + 1) * TILE]
                acc[2 * n + k, rr, :] = vk if off == 0 else acc[2 * n + k, rr, :] + vk

        lhs = jnp.concatenate(
            [cat[2 * (4 * i + yy) + k] for i in range(4) for k in range(2)], axis=1
        )
        for w, acc in ((wg, acc_g), (wu, acc_u)):
            rhs = jnp.concatenate([w[4 * i + yy, :, cols] for i in range(4)], axis=0)
            total(acc, jnp.dot(lhs, rhs, preferred_element_type=jnp.float32))
        lhs = jnp.concatenate([cat[GB + 8 * xx + k] for k in range(8)], axis=1)
        total(acc_h, lax.dot_general(lhs, wd[xx, cols, :], NT, preferred_element_type=jnp.float32))

    def pointwise(h):
        cat = cats[h]

        def body(f, _):
            for r in range(CHUNKS[h] // 64):
                rows = pl.ds(r * 64, 64)
                g, u, hg = acc_g[f, rows, :], acc_u[f, rows, :], acc_h[f, rows, :]
                s = 1.0 / (1.0 + jnp.exp(-g))
                gs = g * s
                cat[HB + f, rows, :] = (gs * u).astype(jnp.bfloat16)
                cat[GGB + f, rows, :] = (hg * u * s * (1.0 + g * (1.0 - s))).astype(jnp.bfloat16)
                cat[GUB + f, rows, :] = (hg * gs).astype(jnp.bfloat16)
            return 0

        lax.fori_loop(0, 6, body, 0)

    def partial(h, off, half):
        cat = cats[h]
        yy = mod4(cy + off)
        at = [4 * i + yy for i in (2 * half, 2 * half + 1)]
        lhs = jnp.concatenate(
            [jnp.concatenate([wg[t], wu[t]], axis=1) for t in at], axis=0
        )
        rhs = jnp.concatenate([cat[GGB + k] for k in range(12)], axis=1)
        v = lax.dot_general(lhs, rhs, NT, preferred_element_type=jnp.float32)
        v = v.astype(jnp.bfloat16)
        for i, t in enumerate(at):
            ps[h][t] = v[256 * i : 256 * (i + 1)]

    def rs(h, p):
        fx = p == 1
        c1, c2 = (cx, cy) if fx else (cy, cx)
        buf = ps[h]
        r0 = p * 128
        full, low, up = pl.ds(r0, 128), pl.ds(r0, 64), pl.ds(r0 + 64, 64)

        def dev(d1, d2):
            return (dp, tensor_at(fx, mod4(c1 + d1), mod4(c2 + d2)))

        def blk(d1, d2):
            return tensor_at(fx, mod4(c1 + d1), mod4(c2 + d2))

        def put(idx, d1, d2, rows, dst, e1, e2):
            send(buf.at[blk(d1, d2), rows, :], dst, rs_s.at[h, p, idx], rs_r.at[h, p, idx], dev(e1, e2))

        def got(idx, dst):
            rcopy(dst, dst, rs_s.at[h, p, idx], rs_r.at[h, p, idx], dev(1, 0)).wait_recv()

        def add(d1, d2, rows, *terms):
            b = blk(d1, d2)
            v = buf[b, rows, :].astype(jnp.float32)
            for ref in terms:
                v = v + ref[...].astype(jnp.float32)
            return b, v

        def addto(d1, d2, rows, *terms):
            b, v = add(d1, d2, rows, *terms)
            buf[b, rows, :] = v.astype(jnp.bfloat16)

        R1 = [[r1[h].at[p, j, k] for k in range(2)] for j in range(4)]
        R2 = [[r2[h].at[p, j, k] for k in range(2)] for j in range(4)]
        R3 = [r3[h].at[p, k] for k in range(2)]
        R4 = [r4[h].at[p, k] for k in range(2)]

        def s1(j):
            put(4 * j, 2, OFF2[j], low, R1[j][0], 1, 0)
            put(4 * j + 1, 2, OFF2[j], up, R1[j][1], -1, 0)

        def t1(j):
            got(4 * j, R1[j][0])
            addto(1, OFF2[j], low, R1[j][0])
            put(4 * j + 2, 1, OFF2[j], full, R2[j][0], 1, 0)
            got(4 * j + 1, R1[j][1])
            addto(-1, OFF2[j], up, R1[j][1])
            put(4 * j + 3, -1, OFF2[j], full, R2[j][1], -1, 0)

        def t2(j):
            got(4 * j + 2, R2[j][0])
            got(4 * j + 3, R2[j][1])
            addto(0, OFF2[j], full, R2[j][0], R2[j][1])
            if j == 0:
                put(16, 0, 2, low, R3[0], 0, 1)
                put(17, 0, 2, up, R3[1], 0, -1)

        def t3():
            got(16, R3[0])
            addto(0, 1, low, R3[0])
            put(18, 0, 1, full, R4[0], 0, 1)
            got(17, R3[1])
            addto(0, -1, up, R3[1])
            put(19, 0, -1, full, R4[1], 0, -1)

        def t4():
            got(18, R4[0])
            got(19, R4[1])
            _, v = add(0, 0, full, R4[0], R4[1])
            rows, cols = pl.ds(STARTS[h], CHUNKS[h]), pl.ds(r0, 128)
            ox[rows, cols] = v.T.astype(jnp.bfloat16)
            put_out(ox.at[rows, cols], out_x.at[rows, cols], 2 * h + p)

        return s1, t1, t2, t3, t4

    RS = [[rs(h, p) for p in range(2)] for h in range(NC)]

    def rs_step(h, k, *a):
        for p in range(2):
            RS[h][p][k](*a)

    UN = 4

    squares = {}

    def tiles_of(h, q0, q1):
        cat, ne = cats[h], NSEQ[h]

        def body(q, carry):
            sq = list(carry)
            for i in range(UN):
                s = q * UN + i
                f, m, kd = sf[s], sm[s], sk[s]
                live = jnp.where(s < lc[0], 1.0, 0.0).astype(jnp.float32)
                li = jnp.where(kd == 2, HB + f, XB + m)
                ri = jnp.where(kd == 0, GGB + f, jnp.where(kd == 1, GUB + f, GB + m))
                for e in range(ne):
                    rows = pl.ds(e * LEN, LEN)
                    v = lax.dot_general(
                        cat[li, rows, :], cat[ri, rows, :], TN, preferred_element_type=jnp.float32
                    )
                    v = v * live
                    tiles[SEQ0[h] + e, s] = v
                    sq[e] = sq[e] + jnp.sum((v * v).reshape(16, 8, TILE), axis=0)
            return tuple(sq)

        z = jnp.zeros((8, TILE), jnp.float32)
        sq = lax.fori_loop(q0, q1, body, squares.pop(h, (z,) * ne))
        if q1 < SLOTS // UN:
            squares[h] = sq
            return
        for e in range(ne):
            nr[h, me, pl.ds(e, 1), :] = jnp.sum(sq[e], axis=0, keepdims=True)

    def norm_send(h):
        for k in range(1, 16):
            r = nr.at[h, me]
            send(r, r, nr_s.at[h, k], nr_r.at[h, k], (dp, lax.rem(me + k, 16)))

    def norm_wait(h):
        for k in range(1, 16):
            src = nr.at[h, lax.rem(me + 16 - k, 16)]
            rcopy(src, src, nr_s.at[h, k], nr_r.at[h, k], (dp, lax.rem(me + k, 16))).wait_recv()
        tot = nr[h, 0]
        for k in range(1, 16):
            tot = tot + nr[h, k]
        tot = jnp.sum(tot, axis=1, keepdims=True)
        clip = jnp.minimum(1.0, BOUND / jnp.sqrt(tot + 1e-06))
        clip = jnp.broadcast_to(clip, (8, TILE))
        return [clip[e : e + 1, :] for e in range(NSEQ[h])]

    def fold(cl):
        def body(s, _):
            v = cl[0] * tiles[0, s]
            for e in range(1, len(cl)):
                v = v + cl[e] * tiles[e, s]
            tiles[0, s] = v
            return 0

        lax.fori_loop(0, SLOTS, body, 0)

    partner = (cz * 2 + 1 - cc, me)
    terms = [0] + [SEQ0[-1] + e for e in range(NSEQ[-1])]

    def rows_of(z, c):
        return pl.ds(pl.multiple_of((2 * z + c) * 16, 16), 16)

    def to_partner(k):
        def body(s, _):
            for z in range(4):
                xs[k, z, s] = tiles[terms[k], s, rows_of(z, 1 - cc), :].astype(jnp.bfloat16)
            return 0

        lax.fori_loop(0, SLOTS, body, 0)
        send(xs.at[k], xr.at[k], x_s.at[k], x_r.at[k], partner)

    def clip_to_partner(cl):
        for e in range(NSEQ[-1]):
            cs[pl.ds(e, 1), :] = cl[e]
        send(cs, cr, c_s.at[0], c_r.at[0], partner)

    def partner_clip():
        rcopy(cr, cr, c_s.at[0], c_r.at[0], partner).wait_recv()
        return [cr[pl.ds(e, 1), :] for e in range(NSEQ[-1])]

    def from_partner(k):
        rcopy(xr.at[k], xr.at[k], x_s.at[k], x_r.at[k], partner).wait_recv()

    def combined(z, s, cl, pcl):
        v = tiles[0, s, rows_of(z, cc), :] + xr[0, z, s].astype(jnp.float32)
        for e in range(NSEQ[-1]):
            v = v + cl[e] * tiles[terms[e + 1], s, rows_of(z, cc), :]
            v = v + pcl[e] * xr[e + 1, z, s].astype(jnp.float32)
        return v

    HALF = (pl.ds(0, SLOTS // 2), pl.ds(SLOTS // 2, SLOTS // 2))

    def combine(d, half, cl, pcl):
        z = mod4(cz + d)

        def body(i, _):
            s = half * (SLOTS // 2) + i
            zs[z, s] = combined(z, s, cl, pcl).astype(jnp.bfloat16)
            return 0

        lax.fori_loop(0, SLOTS // 2, body, 0)

    def zput(idx, d_block, half, dst, d):
        send(
            zs.at[mod4(cz + d_block), HALF[half]],
            zr.at[dst, HALF[half]],
            z_s.at[idx],
            z_r.at[idx],
            (mod4(cz + d) * 2 + cc, me),
        )

    def zgot(idx, dst, half):
        r = zr.at[dst, HALF[half]]
        rcopy(r, r, z_s.at[idx], z_r.at[idx], (mod4(cz + 1) * 2 + cc, me)).wait_recv()

    def zadd(d_block, half, src):
        z = mod4(cz + d_block)
        v = zs[z, HALF[half]].astype(jnp.float32) + zr[src, HALF[half]].astype(jnp.float32)
        zs[z, HALF[half]] = v.astype(jnp.bfloat16)

    def z_start(cl, pcl):
        combine(2, 0, cl, pcl)
        zput(0, 2, 0, 0, 1)
        combine(2, 1, cl, pcl)
        zput(1, 2, 1, 1, -1)
        combine(1, 1, cl, pcl)
        zput(2, 1, 1, 2, 1)
        combine(-1, 0, cl, pcl)
        zput(3, -1, 0, 3, -1)
        combine(1, 0, cl, pcl)
        combine(-1, 1, cl, pcl)

    def z_pass():
        zgot(0, 0, 0)
        zadd(1, 0, 0)
        zput(4, 1, 0, 2, 1)
        zgot(1, 1, 1)
        zadd(-1, 1, 1)
        zput(5, -1, 1, 3, -1)

    def z_own(cl, pcl):
        def body(s, _):
            ob[s] = combined(cz, s, cl, pcl)
            return 0

        lax.fori_loop(0, SLOTS, body, 0)

    def z_end(half):
        zgot(2 if half else 4, 2, half)
        zgot(5 if half else 3, 3, half)
        sl = HALF[half]
        ob[sl] = ob[sl] + zr[2, sl].astype(jnp.float32) + zr[3, sl].astype(jnp.float32)
        put_out(ob.at[sl], out_b.at[sl], 2 * NC + half)

    for c in own[:4]:
        c.wait()
    AG[0][0][0]()
    AG[0][1][0]()
    for c in own[4:]:
        c.wait()
    nr[:, me] = jnp.zeros((NC, 8, TILE), jnp.float32)
    cs[...] = jnp.zeros((8, TILE), jnp.float32)
    AG[0][0][2]()
    AG[0][0][1]()
    AG[0][1][1]()
    AG[0][1][2]()
    AG[0][0][3]()
    AG[0][0][4](0)
    AG[0][0][4](2)
    AG[0][1][4](0)
    for c in wcopies:
        c.wait()
    AG[0][1][4](1)
    AG[0][1][3]()
    AG[0][0][4](3)
    AG[0][1][4](2)
    fwd(0, 0, 2)
    AG[0][0][4](1)
    fwd(0, 0, 0)
    AG[1][0][0]()
    AG[0][1][5](0)
    AG[0][0][5](2)
    AG[0][1][4](3)
    fwd(0, 0, 1)
    AG[1][1][0]()
    fwd(0, 1, 0)
    fwd(0, 1, 2)
    fwd(0, 1, 1)
    AG[0][0][5](3)
    fwd(0, -1, 2)
    AG[0][0][5](0)
    AG[0][0][5](1)
    fwd(0, -1, 1)
    AG[1][0][1]()
    fwd(0, -1, 0)
    AG[0][1][5](2)
    AG[0][1][5](3)
    AG[0][1][5](1)
    fwd(0, 2, 0)
    AG[1][0][2]()
    fwd(0, 2, 1)
    fwd(0, 2, 2)
    AG[1][1][1]()
    pointwise(0)
    tiles_of(0, 0, 6)
    AG[1][1][2]()
    AG[1][1][4](0)
    tiles_of(0, 6, 12)
    AG[1][0][3]()
    norm_send(0)
    partial(0, OFF2[0], 0)
    partial(0, OFF2[0], 1)
    RS[0][0][0](0)
    partial(0, OFF2[1], 0)
    partial(0, OFF2[1], 1)
    RS[0][1][0](0)
    RS[0][0][0](3)
    partial(0, OFF2[2], 0)
    partial(0, OFF2[2], 1)
    AG[1][0][4](0)
    AG[1][1][3]()
    partial(0, OFF2[3], 0)
    partial(0, OFF2[3], 1)
    AG[1][0][4](2)
    fwd(1, 0, 0)
    fwd(1, 0, 1)
    AG[1][0][4](1)
    AG[1][0][4](3)
    early = norm_wait(0)
    AG[1][1][4](2)
    AG[1][1][4](1)
    RS[0][0][1](0)
    fold(early)
    RS[0][0][0](1)
    RS[0][0][1](3)
    fwd(1, 0, 2)
    AG[1][1][4](3)
    fwd(1, 1, 2)
    AG[1][1][5](0)
    fwd(1, 1, 1)
    fwd(1, -1, 2)
    fwd(1, -1, 1)
    fwd(1, -1, 0)
    RS[0][1][0](1)
    AG[1][0][5](0)
    AG[1][1][5](1)
    RS[0][1][0](3)
    RS[0][0][0](2)
    RS[0][1][0](2)
    RS[0][1][1](0)
    fwd(1, 1, 0)
    AG[1][0][5](1)
    AG[1][0][5](2)
    AG[1][1][5](2)
    AG[1][0][5](3)
    AG[1][1][5](3)
    fwd(1, 2, 1)
    fwd(1, 2, 2)
    fwd(1, 2, 0)
    pointwise(1)
    partial(1, OFF2[0], 0)
    partial(1, OFF2[0], 1)
    partial(1, OFF2[1], 0)
    partial(1, OFF2[1], 1)
    RS[1][0][0](0)
    RS[1][1][0](0)
    RS[1][0][0](1)
    RS[0][1][1](2)
    RS[1][1][0](1)
    tiles_of(1, 0, 6)
    RS[0][1][1](1)
    RS[0][1][1](3)
    RS[1][0][0](2)
    tiles_of(1, 6, 12)
    norm_send(1)
    RS[1][0][0](3)
    RS[0][0][1](1)
    RS[1][1][1](0)
    partial(1, OFF2[2], 0)
    partial(1, OFF2[2], 1)
    RS[1][0][1](0)
    RS[1][1][0](2)
    RS[0][0][1](2)
    to_partner(1)
    partial(1, OFF2[3], 0)
    partial(1, OFF2[3], 1)
    RS[1][1][0](3)
    to_partner(2)
    RS[0][0][2](0)
    to_partner(0)
    RS[1][1][1](1)
    RS[1][0][1](1)
    clip = norm_wait(1)
    clip_to_partner(clip)
    RS[1][0][1](2)
    RS[1][1][1](2)
    RS[1][0][2](0)
    RS[1][1][2](0)
    RS[0][1][2](0)
    RS[1][1][1](3)
    for k in range(NT1):
        from_partner(k)
    pclip = partner_clip()
    z_start(clip, pclip)
    RS[1][0][1](3)
    RS[0][0][2](2)
    RS[0][0][2](1)
    RS[0][0][3]()
    RS[0][1][2](1)
    RS[1][1][2](2)
    RS[1][1][2](1)
    RS[1][0][2](2)
    RS[1][1][3]()
    RS[1][0][2](1)
    RS[0][1][2](2)
    RS[1][0][3]()
    RS[0][1][3]()
    z_pass()
    z_own(clip, pclip)
    RS[1][0][2](3)
    RS[1][1][2](3)
    RS[0][0][2](3)
    RS[0][1][2](3)
    RS[0][0][4]()
    RS[1][0][4]()
    RS[1][1][4]()
    RS[0][1][4]()
    z_end(0)
    z_end(1)
    for c in sends:
        c.wait_send()
    for c in outs:
        c.wait()


def hand_out(x, b, out_x, out_b, vx, vb, sem):
    ins = [pltpu.make_async_copy(x, vx, sem.at[0]), pltpu.make_async_copy(b, vb, sem.at[1])]
    outs = [pltpu.make_async_copy(vx, out_x, sem.at[2]), pltpu.make_async_copy(vb, out_b, sem.at[3])]
    for c in ins:
        c.start()
    for i, o in zip(ins, outs):
        i.wait()
        o.start()
    for o in outs:
        o.wait()


def per_device(
    tokens,
    out_grad,
    gate_weight,
    up_weight,
    down_weight,
    slot_ffn_block,
    slot_model_block,
    slot_kind,
    live_count,
):
    bf, f32 = jnp.bfloat16, jnp.float32
    anyspec = pl.BlockSpec(memory_space=pl.ANY)
    smem = pl.BlockSpec(memory_space=pltpu.SMEM)
    dma = pltpu.SemaphoreType.DMA
    grad_x, grad_b = pl.pallas_call(
        kernel,
        out_shape=(
            jax.ShapeDtypeStruct((512, 256), bf),
            jax.ShapeDtypeStruct((SLOTS, 16, TILE), f32),
        ),
        in_specs=[anyspec] * 5 + [smem] * 4,
        out_specs=(anyspec, anyspec),
        scratch_shapes=[
            [pltpu.VMEM((BLOCKS, r, TILE), bf) for r in CHUNKS],
            pltpu.VMEM((16, 256, 768), bf),
            pltpu.VMEM((16, 256, 768), bf),
            pltpu.VMEM((4, 768, 1024), bf),
            pltpu.VMEM((6, max(CHUNKS), TILE), f32),
            pltpu.VMEM((6, max(CHUNKS), TILE), f32),
            pltpu.VMEM((6, max(CHUNKS), TILE), f32),
            [pltpu.VMEM((16, 256, r), bf) for r in CHUNKS],
            [pltpu.VMEM((2, 4, 2, 64, r), bf) for r in CHUNKS],
            [pltpu.VMEM((2, 4, 2, 128, r), bf) for r in CHUNKS],
            [pltpu.VMEM((2, 2, 64, r), bf) for r in CHUNKS],
            [pltpu.VMEM((2, 2, 128, r), bf) for r in CHUNKS],
            pltpu.VMEM((4, SLOTS, TILE, TILE), f32),
            pltpu.VMEM((NC, 16, 8, TILE), f32),
            pltpu.VMEM((NT1, 4, SLOTS, 16, TILE), bf),
            pltpu.VMEM((NT1, 4, SLOTS, 16, TILE), bf),
            pltpu.VMEM((8, TILE), f32),
            pltpu.VMEM((8, TILE), f32),
            pltpu.VMEM((4, SLOTS, 16, TILE), bf),
            pltpu.VMEM((4, SLOTS, 16, TILE), bf),
            dma((NC, 2, 2)),
            dma((6,)),
            dma((NC, 2, 20)),
            dma((NC, 2, 20)),
            dma((NC, 2, 20)),
            dma((NC, 2, 20)),
            dma((NC, 16)),
            dma((NC, 16)),
            dma((NT1,)),
            dma((NT1,)),
            dma((1,)),
            dma((1,)),
            dma((6,)),
            dma((6,)),
            dma((2 * NC + 2,)),
            pltpu.VMEM((512, 256), bf),
            pltpu.VMEM((SLOTS, 16, TILE), f32),
        ],
        compiler_params=pltpu.CompilerParams(
            collective_id=0, has_side_effects=True, vmem_limit_bytes=62 << 20
        ),
        cost_estimate=pl.CostEstimate(
            flops=17_000_000_000, bytes_accessed=20_000_000, transcendentals=400_000
        ),
    )(
        tokens,
        out_grad,
        gate_weight.reshape(16, 256, 768),
        up_weight.reshape(16, 256, 768),
        down_weight,
        slot_ffn_block,
        slot_model_block,
        slot_kind,
        live_count,
    )
    return pl.pallas_call(
        hand_out,
        out_shape=(
            jax.ShapeDtypeStruct((512, 256), bf),
            jax.ShapeDtypeStruct((SLOTS, 16, TILE), f32),
        ),
        in_specs=[anyspec] * 2,
        out_specs=(anyspec, anyspec),
        scratch_shapes=[
            pltpu.VMEM((512, 256), bf),
            pltpu.VMEM((SLOTS, 16, TILE), f32),
            dma((4,)),
        ],
    )(grad_x, grad_b)


def solution(mesh):
    return jax.shard_map(
        per_device,
        mesh=mesh,
        in_specs=(
            P("dp", "tensor"),
            P("dp", "tensor"),
            P(None, "tensor"),
            P(None, "tensor"),
            P("tensor", None),
            P("tensor"),
            P("tensor"),
            P("tensor"),
            P("tensor"),
        ),
        out_specs=(P("dp", "tensor"), P("tensor", "dp", None)),
        check_vma=False,
    )
```

```python
import math

import jax
import jax.numpy as jnp
from jax import lax
from jax.experimental import pallas as pl
from jax.experimental.pallas import tpu as pltpu
from jax.sharding import PartitionSpec as P

TILE = 128
LEN = 128
CHUNKS = (256, 256)
STARTS = tuple(sum(CHUNKS[:i]) for i in range(len(CHUNKS)))
NC = len(CHUNKS)
SEQ0 = tuple(v // LEN for v in STARTS)
NSEQ = tuple(v // LEN for v in CHUNKS)
SLOTS = 48
NX = 4
XB, GB, HB, GGB, GUB = 0, 32, 64, 70, 76
BLOCKS = 82
OFF = (0, -1, 1, 2)
OFF2 = (2, 1, -1, 0)
MESH = pl.DeviceIdType.MESH
BOUND = 0.33 * TILE * math.sqrt(LEN * 768)
NT = (((1,), (1,)), ((), ()))
TN = (((0,), (0,)), ((), ()))
NT1 = 1 + NSEQ[-1]


def mod4(v):
    return lax.rem(v + 8, 4)


def kernel(
    tok,
    og,
    gw,
    uw,
    dw,
    sf,
    sm,
    sk,
    lc,
    out_x,
    out_b,
    cats,
    wg,
    wu,
    wd,
    acc_g,
    acc_u,
    acc_h,
    ps,
    r1,
    r2,
    r3,
    r4,
    tiles,
    nr,
    xs,
    xr,
    cs,
    cr,
    zs,
    zr,
    own_sem,
    w_sem,
    ag_s,
    ag_r,
    rs_s,
    rs_r,
    nr_s,
    nr_r,
    x_s,
    x_r,
    c_s,
    c_r,
    z_s,
    z_r,
    o_sem,
    ox,
    ob,
):
    dp = lax.axis_index("dp")
    me = lax.axis_index("tensor")
    cx, cy = me // 4, lax.rem(me, 4)
    cz, cc = dp // 2, lax.rem(dp, 2)
    sends = []

    barrier = pltpu.get_barrier_semaphore()
    z_next = [(mod4(cz + d) * 2 + cc, me) for d in (1, -1)]
    near = [
        (dp, mod4(cx + 1) * 4 + cy),
        (dp, mod4(cx - 1) * 4 + cy),
        (dp, cx * 4 + mod4(cy + 1)),
        (dp, cx * 4 + mod4(cy - 1)),
        (cz * 2 + 1 - cc, me),
    ] + z_next
    for dev in near:
        pl.semaphore_signal(barrier, inc=1, device_id=dev, device_id_type=MESH)

    own = []
    for h in range(NC):
        for arr, src in ((0, tok), (1, og)):
            for k in range(2):
                c = pltpu.make_async_copy(
                    src.at[pl.ds(STARTS[h], CHUNKS[h]), pl.ds(k * TILE, TILE)],
                    cats[h].at[32 * arr + 2 * me + k],
                    own_sem.at[h, arr, k],
                )
                c.start()
                own.append(c)
    wcopies = [
        pltpu.make_async_copy(gw, wg, w_sem.at[0]),
        pltpu.make_async_copy(uw, wu, w_sem.at[1]),
    ] + [
        pltpu.make_async_copy(dw.at[:, pl.ds(1024 * i, 1024)], wd.at[i], w_sem.at[2 + i])
        for i in range(4)
    ]
    for c in wcopies:
        c.start()

    pl.semaphore_wait(barrier, len(near))

    def rcopy(src, dst, ssem, rsem, dev):
        return pltpu.make_async_remote_copy(
            src_ref=src, dst_ref=dst, send_sem=ssem, recv_sem=rsem, device_id=dev, device_id_type=MESH
        )

    def send(src, dst, ssem, rsem, dev):
        c = rcopy(src, dst, ssem, rsem, dev)
        c.start()
        sends.append(c)

    outs = []

    def put_out(src, dst, idx):
        c = pltpu.make_async_copy(src, dst, o_sem.at[idx])
        c.start()
        outs.append(c)

    def tensor_at(first_is_x, a1, a2):
        return a1 * 4 + a2 if first_is_x else a2 * 4 + a1

    def ag(h, arr):
        R = CHUNKS[h]
        fx = arr == 0
        c1, c2 = (cx, cy) if fx else (cy, cx)

        def dev(d1, d2):
            return (dp, tensor_at(fx, mod4(c1 + d1), mod4(c2 + d2)))

        def region(d1, d2, part):
            t = tensor_at(fx, mod4(c1 + d1), mod4(c2 + d2))
            rows = (pl.ds(0, R), pl.ds(0, R // 2), pl.ds(R // 2, R // 2))[part]
            return cats[h].at[pl.ds(32 * arr + 2 * t, 2), rows, :]

        def put(idx, d1, d2, part, e1, e2):
            r = region(d1, d2, part)
            send(r, r, ag_s.at[h, arr, idx], ag_r.at[h, arr, idx], dev(e1, e2))

        def got(idx, d1, d2, part):
            r = region(d1, d2, part)
            rcopy(r, r, ag_s.at[h, arr, idx], ag_r.at[h, arr, idx], dev(1, 0)).wait_recv()

        def start():
            put(0, 0, 0, 0, 1, 0)
            put(1, 0, 0, 0, -1, 0)
            put(4, 0, 0, 0, 0, 1)
            put(5, 0, 0, 0, 0, -1)

        def spread(j):
            put(4 + 4 * j, OFF[j], 0, 0, 0, 1)
            put(5 + 4 * j, OFF[j], 0, 0, 0, -1)

        def e1():
            got(0, -1, 0, 0)
            put(2, -1, 0, 1, 1, 0)
            spread(1)

        def e2():
            got(1, 1, 0, 0)
            put(3, 1, 0, 2, -1, 0)
            spread(2)

        def e3():
            got(2, 2, 0, 1)
            got(3, 2, 0, 2)
            spread(3)

        def e4(j):
            got(4 + 4 * j, OFF[j], -1, 0)
            put(6 + 4 * j, OFF[j], -1, 1, 0, 1)
            got(5 + 4 * j, OFF[j], 1, 0)
            put(7 + 4 * j, OFF[j], 1, 2, 0, -1)

        def e5(j):
            got(6 + 4 * j, OFF[j], 2, 1)
            got(7 + 4 * j, OFF[j], 2, 2)

        return start, e1, e2, e3, e4, e5

    AG = [[ag(h, arr) for arr in range(2)] for h in range(NC)]

    def ag_step(h, k, *a):
        for arr in range(2):
            AG[h][arr][k](*a)

    def fwd(h, off, n):
        cat, rr = cats[h], pl.ds(0, CHUNKS[h])
        yy, xx = mod4(cy + off), mod4(cx + off)
        cols = pl.ds(n * 256, 256)

        def total(acc, v):
            for k in range(2):
                vk = v[:, k * TILE : (k + 1) * TILE]
                acc[2 * n + k, rr, :] = vk if off == 0 else acc[2 * n + k, rr, :] + vk

        lhs = jnp.concatenate(
            [cat[2 * (4 * i + yy) + k] for i in range(4) for k in range(2)], axis=1
        )
        for w, acc in ((wg, acc_g), (wu, acc_u)):
            rhs = jnp.concatenate([w[4 * i + yy, :, cols] for i in range(4)], axis=0)
            total(acc, jnp.dot(lhs, rhs, preferred_element_type=jnp.float32))
        lhs = jnp.concatenate([cat[GB + 8 * xx + k] for k in range(8)], axis=1)
        total(acc_h, lax.dot_general(lhs, wd[xx, cols, :], NT, preferred_element_type=jnp.float32))

    def pointwise(h):
        cat = cats[h]

        def body(f, _):
            for r in range(CHUNKS[h] // 64):
                rows = pl.ds(r * 64, 64)
                g, u, hg = acc_g[f, rows, :], acc_u[f, rows, :], acc_h[f, rows, :]
                s = 1.0 / (1.0 + jnp.exp(-g))
                gs = g * s
                cat[HB + f, rows, :] = (gs * u).astype(jnp.bfloat16)
                cat[GGB + f, rows, :] = (hg * u * s * (1.0 + g * (1.0 - s))).astype(jnp.bfloat16)
                cat[GUB + f, rows, :] = (hg * gs).astype(jnp.bfloat16)
            return 0

        lax.fori_loop(0, 6, body, 0)

    def partial(h, off, half):
        cat = cats[h]
        yy = mod4(cy + off)
        at = [4 * i + yy for i in (2 * half, 2 * half + 1)]
        lhs = jnp.concatenate(
            [jnp.concatenate([wg[t], wu[t]], axis=1) for t in at], axis=0
        )
        rhs = jnp.concatenate([cat[GGB + k] for k in range(12)], axis=1)
        v = lax.dot_general(lhs, rhs, NT, preferred_element_type=jnp.float32)
        v = v.astype(jnp.bfloat16)
        for i, t in enumerate(at):
            ps[h][t] = v[256 * i : 256 * (i + 1)]

    def rs(h, p):
        fx = p == 1
        c1, c2 = (cx, cy) if fx else (cy, cx)
        buf = ps[h]
        r0 = p * 128
        full, low, up = pl.ds(r0, 128), pl.ds(r0, 64), pl.ds(r0 + 64, 64)

        def dev(d1, d2):
            return (dp, tensor_at(fx, mod4(c1 + d1), mod4(c2 + d2)))

        def blk(d1, d2):
            return tensor_at(fx, mod4(c1 + d1), mod4(c2 + d2))

        def put(idx, d1, d2, rows, dst, e1, e2):
            send(buf.at[blk(d1, d2), rows, :], dst, rs_s.at[h, p, idx], rs_r.at[h, p, idx], dev(e1, e2))

        def got(idx, dst):
            rcopy(dst, dst, rs_s.at[h, p, idx], rs_r.at[h, p, idx], dev(1, 0)).wait_recv()

        def add(d1, d2, rows, *terms):
            b = blk(d1, d2)
            v = buf[b, rows, :].astype(jnp.float32)
            for ref in terms:
                v = v + ref[...].astype(jnp.float32)
            return b, v

        def addto(d1, d2, rows, *terms):
            b, v = add(d1, d2, rows, *terms)
            buf[b, rows, :] = v.astype(jnp.bfloat16)

        R1 = [[r1[h].at[p, j, k] for k in range(2)] for j in range(4)]
        R2 = [[r2[h].at[p, j, k] for k in range(2)] for j in range(4)]
        R3 = [r3[h].at[p, k] for k in range(2)]
        R4 = [r4[h].at[p, k] for k in range(2)]

        def s1(j):
            put(4 * j, 2, OFF2[j], low, R1[j][0], 1, 0)
            put(4 * j + 1, 2, OFF2[j], up, R1[j][1], -1, 0)

        def t1(j):
            got(4 * j, R1[j][0])
            addto(1, OFF2[j], low, R1[j][0])
            put(4 * j + 2, 1, OFF2[j], full, R2[j][0], 1, 0)
            got(4 * j + 1, R1[j][1])
            addto(-1, OFF2[j], up, R1[j][1])
            put(4 * j + 3, -1, OFF2[j], full, R2[j][1], -1, 0)

        def t2(j):
            got(4 * j + 2, R2[j][0])
            got(4 * j + 3, R2[j][1])
            addto(0, OFF2[j], full, R2[j][0], R2[j][1])
            if j == 0:
                put(16, 0, 2, low, R3[0], 0, 1)
                put(17, 0, 2, up, R3[1], 0, -1)

        def t3():
            got(16, R3[0])
            addto(0, 1, low, R3[0])
            put(18, 0, 1, full, R4[0], 0, 1)
            got(17, R3[1])
            addto(0, -1, up, R3[1])
            put(19, 0, -1, full, R4[1], 0, -1)

        def t4():
            got(18, R4[0])
            got(19, R4[1])
            _, v = add(0, 0, full, R4[0], R4[1])
            rows, cols = pl.ds(STARTS[h], CHUNKS[h]), pl.ds(r0, 128)
            ox[rows, cols] = v.T.astype(jnp.bfloat16)
            put_out(ox.at[rows, cols], out_x.at[rows, cols], 2 * h + p)

        return s1, t1, t2, t3, t4

    RS = [[rs(h, p) for p in range(2)] for h in range(NC)]

    def rs_step(h, k, *a):
        for p in range(2):
            RS[h][p][k](*a)

    UN = 4

    squares = {}

    def tiles_of(h, q0, q1):
        cat, ne = cats[h], NSEQ[h]

        def body(q, carry):
            sq = list(carry)
            for i in range(UN):
                s = q * UN + i
                f, m, kd = sf[s], sm[s], sk[s]
                live = jnp.where(s < lc[0], 1.0, 0.0).astype(jnp.float32)
                li = jnp.where(kd == 2, HB + f, XB + m)
                ri = jnp.where(kd == 0, GGB + f, jnp.where(kd == 1, GUB + f, GB + m))
                for e in range(ne):
                    rows = pl.ds(e * LEN, LEN)
                    v = lax.dot_general(
                        cat[li, rows, :], cat[ri, rows, :], TN, preferred_element_type=jnp.float32
                    )
                    v = v * live
                    tiles[SEQ0[h] + e, s] = v
                    sq[e] = sq[e] + jnp.sum((v * v).reshape(16, 8, TILE), axis=0)
            return tuple(sq)

        z = jnp.zeros((8, TILE), jnp.float32)
        sq = lax.fori_loop(q0, q1, body, squares.pop(h, (z,) * ne))
        if q1 < SLOTS // UN:
            squares[h] = sq
            return
        for e in range(ne):
            nr[h, me, pl.ds(e, 1), :] = jnp.sum(sq[e], axis=0, keepdims=True)

    def norm_send(h):
        for k in range(1, 16):
            r = nr.at[h, me]
            send(r, r, nr_s.at[h, k], nr_r.at[h, k], (dp, lax.rem(me + k, 16)))

    def norm_wait(h):
        for k in range(1, 16):
            src = nr.at[h, lax.rem(me + 16 - k, 16)]
            rcopy(src, src, nr_s.at[h, k], nr_r.at[h, k], (dp, lax.rem(me + k, 16))).wait_recv()
        tot = nr[h, 0]
        for k in range(1, 16):
            tot = tot + nr[h, k]
        tot = jnp.sum(tot, axis=1, keepdims=True)
        clip = jnp.minimum(1.0, BOUND / jnp.sqrt(tot + 1e-06))
        clip = jnp.broadcast_to(clip, (8, TILE))
        return [clip[e : e + 1, :] for e in range(NSEQ[h])]

    def fold(cl):
        def body(s, _):
            v = cl[0] * tiles[0, s]
            for e in range(1, len(cl)):
                v = v + cl[e] * tiles[e, s]
            tiles[0, s] = v
            return 0

        lax.fori_loop(0, SLOTS, body, 0)

    partner = (cz * 2 + 1 - cc, me)
    terms = [0] + [SEQ0[-1] + e for e in range(NSEQ[-1])]

    def rows_of(z, c):
        return pl.ds(pl.multiple_of((2 * z + c) * 16, 16), 16)

    def to_partner(k):
        def body(q, _):
            for i in range(UN):
                s = q * UN + i
                for z in range(4):
                    xs[k, z, s] = tiles[terms[k], s, rows_of(z, 1 - cc), :].astype(jnp.bfloat16)
            return 0

        lax.fori_loop(0, SLOTS // UN, body, 0)
        send(xs.at[k], xr.at[k], x_s.at[k], x_r.at[k], partner)

    def clip_to_partner(cl):
        for e in range(NSEQ[-1]):
            cs[pl.ds(e, 1), :] = cl[e]
        send(cs, cr, c_s.at[0], c_r.at[0], partner)

    def partner_clip():
        rcopy(cr, cr, c_s.at[0], c_r.at[0], partner).wait_recv()
        return [cr[pl.ds(e, 1), :] for e in range(NSEQ[-1])]

    def from_partner(k):
        rcopy(xr.at[k], xr.at[k], x_s.at[k], x_r.at[k], partner).wait_recv()

    def combined(z, s, cl, pcl):
        v = tiles[0, s, rows_of(z, cc), :] + xr[0, z, s].astype(jnp.float32)
        for e in range(NSEQ[-1]):
            v = v + cl[e] * tiles[terms[e + 1], s, rows_of(z, cc), :]
            v = v + pcl[e] * xr[e + 1, z, s].astype(jnp.float32)
        return v

    HALF = (pl.ds(0, SLOTS // 2), pl.ds(SLOTS // 2, SLOTS // 2))

    def combine(d, half, cl, pcl):
        z = mod4(cz + d)

        def body(q, _):
            for i in range(UN):
                s = half * (SLOTS // 2) + q * UN + i
                zs[z, s] = combined(z, s, cl, pcl).astype(jnp.bfloat16)
            return 0

        lax.fori_loop(0, SLOTS // 2 // UN, body, 0)

    def zput(idx, d_block, half, dst, d):
        send(
            zs.at[mod4(cz + d_block), HALF[half]],
            zr.at[dst, HALF[half]],
            z_s.at[idx],
            z_r.at[idx],
            (mod4(cz + d) * 2 + cc, me),
        )

    def zgot(idx, dst, half):
        r = zr.at[dst, HALF[half]]
        rcopy(r, r, z_s.at[idx], z_r.at[idx], (mod4(cz + 1) * 2 + cc, me)).wait_recv()

    def zadd(d_block, half, src):
        z = mod4(cz + d_block)
        v = zs[z, HALF[half]].astype(jnp.float32) + zr[src, HALF[half]].astype(jnp.float32)
        zs[z, HALF[half]] = v.astype(jnp.bfloat16)

    def z_start(cl, pcl):
        combine(2, 0, cl, pcl)
        zput(0, 2, 0, 0, 1)
        combine(2, 1, cl, pcl)
        zput(1, 2, 1, 1, -1)
        combine(1, 1, cl, pcl)
        zput(2, 1, 1, 2, 1)
        combine(-1, 0, cl, pcl)
        zput(3, -1, 0, 3, -1)
        combine(1, 0, cl, pcl)
        combine(-1, 1, cl, pcl)

    def z_pass():
        zgot(0, 0, 0)
        zadd(1, 0, 0)
        zput(4, 1, 0, 2, 1)
        zgot(1, 1, 1)
        zadd(-1, 1, 1)
        zput(5, -1, 1, 3, -1)

    def z_own(cl, pcl):
        def body(q, _):
            for i in range(UN):
                s = q * UN + i
                ob[s] = combined(cz, s, cl, pcl)
            return 0

        lax.fori_loop(0, SLOTS // UN, body, 0)

    def z_end(half):
        zgot(2 if half else 4, 2, half)
        zgot(5 if half else 3, 3, half)
        sl = HALF[half]
        ob[sl] = ob[sl] + zr[2, sl].astype(jnp.float32) + zr[3, sl].astype(jnp.float32)
        put_out(ob.at[sl], out_b.at[sl], 2 * NC + half)

    for c in own[:4]:
        c.wait()
    AG[0][0][0]()
    AG[0][1][0]()
    for c in own[4:]:
        c.wait()
    nr[:, me] = jnp.zeros((NC, 8, TILE), jnp.float32)
    cs[...] = jnp.zeros((8, TILE), jnp.float32)
    AG[0][0][2]()
    AG[0][0][1]()
    AG[0][1][1]()
    AG[0][1][2]()
    AG[0][0][3]()
    AG[0][0][4](0)
    AG[0][0][4](2)
    AG[0][1][4](0)
    for c in wcopies:
        c.wait()
    AG[0][1][4](1)
    AG[0][1][3]()
    AG[0][0][4](3)
    AG[0][1][4](2)
    fwd(0, 0, 2)
    AG[0][0][4](1)
    fwd(0, 0, 0)
    AG[1][0][0]()
    AG[0][1][5](0)
    AG[0][0][5](2)
    AG[0][1][4](3)
    fwd(0, 0, 1)
    AG[1][1][0]()
    fwd(0, 1, 0)
    fwd(0, 1, 2)
    fwd(0, 1, 1)
    AG[0][0][5](3)
    fwd(0, -1, 2)
    AG[0][0][5](0)
    AG[0][0][5](1)
    fwd(0, -1, 1)
    AG[1][0][1]()
    fwd(0, -1, 0)
    AG[0][1][5](2)
    AG[0][1][5](3)
    AG[0][1][5](1)
    fwd(0, 2, 0)
    AG[1][0][2]()
    fwd(0, 2, 1)
    fwd(0, 2, 2)
    AG[1][1][1]()
    pointwise(0)
    tiles_of(0, 0, 6)
    AG[1][1][2]()
    AG[1][1][4](0)
    tiles_of(0, 6, 12)
    AG[1][0][3]()
    norm_send(0)
    partial(0, OFF2[0], 0)
    partial(0, OFF2[0], 1)
    RS[0][0][0](0)
    partial(0, OFF2[1], 0)
    partial(0, OFF2[1], 1)
    RS[0][1][0](0)
    RS[0][0][0](3)
    partial(0, OFF2[2], 0)
    partial(0, OFF2[2], 1)
    AG[1][0][4](0)
    AG[1][1][3]()
    partial(0, OFF2[3], 0)
    partial(0, OFF2[3], 1)
    AG[1][0][4](2)
    fwd(1, 0, 0)
    fwd(1, 0, 1)
    AG[1][0][4](1)
    AG[1][0][4](3)
    early = norm_wait(0)
    AG[1][1][4](2)
    AG[1][1][4](1)
    RS[0][0][1](0)
    fold(early)
    RS[0][0][0](1)
    RS[0][0][1](3)
    fwd(1, 0, 2)
    AG[1][1][4](3)
    fwd(1, 1, 2)
    AG[1][1][5](0)
    fwd(1, 1, 1)
    fwd(1, -1, 2)
    fwd(1, -1, 1)
    fwd(1, -1, 0)
    RS[0][1][0](1)
    AG[1][0][5](0)
    AG[1][1][5](1)
    RS[0][1][0](3)
    RS[0][0][0](2)
    RS[0][1][0](2)
    RS[0][1][1](0)
    fwd(1, 1, 0)
    AG[1][0][5](1)
    AG[1][0][5](2)
    AG[1][1][5](2)
    AG[1][0][5](3)
    AG[1][1][5](3)
    fwd(1, 2, 1)
    fwd(1, 2, 2)
    fwd(1, 2, 0)
    pointwise(1)
    partial(1, OFF2[0], 0)
    partial(1, OFF2[0], 1)
    partial(1, OFF2[1], 0)
    partial(1, OFF2[1], 1)
    RS[1][0][0](0)
    RS[1][1][0](0)
    RS[1][0][0](1)
    RS[0][1][1](2)
    RS[1][1][0](1)
    tiles_of(1, 0, 6)
    RS[0][1][1](1)
    RS[0][1][1](3)
    RS[1][0][0](2)
    tiles_of(1, 6, 12)
    norm_send(1)
    RS[1][0][0](3)
    RS[0][0][1](1)
    RS[1][1][1](0)
    partial(1, OFF2[2], 0)
    partial(1, OFF2[2], 1)
    RS[1][0][1](0)
    RS[1][1][0](2)
    RS[0][0][1](2)
    to_partner(1)
    partial(1, OFF2[3], 0)
    partial(1, OFF2[3], 1)
    RS[1][1][0](3)
    to_partner(2)
    RS[0][0][2](0)
    to_partner(0)
    RS[1][1][1](1)
    RS[1][0][1](1)
    clip = norm_wait(1)
    clip_to_partner(clip)
    RS[1][0][1](2)
    RS[1][1][1](2)
    RS[1][0][2](0)
    RS[1][1][2](0)
    RS[0][1][2](0)
    RS[1][1][1](3)
    for k in range(NT1):
        from_partner(k)
    pclip = partner_clip()
    z_start(clip, pclip)
    RS[1][0][1](3)
    RS[0][0][2](2)
    RS[0][0][2](1)
    RS[0][0][3]()
    RS[0][1][2](1)
    RS[1][1][2](2)
    RS[1][1][2](1)
    RS[1][0][2](2)
    RS[1][1][3]()
    RS[1][0][2](1)
    RS[0][1][2](2)
    RS[1][0][3]()
    RS[0][1][3]()
    z_pass()
    z_own(clip, pclip)
    RS[1][0][2](3)
    RS[1][1][2](3)
    RS[0][0][2](3)
    RS[0][1][2](3)
    RS[0][0][4]()
    RS[1][0][4]()
    RS[1][1][4]()
    RS[0][1][4]()
    z_end(0)
    z_end(1)
    for c in sends:
        c.wait_send()
    for c in outs:
        c.wait()


def hand_out(x, b, out_x, out_b, vx, vb, sem):
    ins = [pltpu.make_async_copy(x, vx, sem.at[0]), pltpu.make_async_copy(b, vb, sem.at[1])]
    outs = [pltpu.make_async_copy(vx, out_x, sem.at[2]), pltpu.make_async_copy(vb, out_b, sem.at[3])]
    for c in ins:
        c.start()
    for i, o in zip(ins, outs):
        i.wait()
        o.start()
    for o in outs:
        o.wait()


def per_device(
    tokens,
    out_grad,
    gate_weight,
    up_weight,
    down_weight,
    slot_ffn_block,
    slot_model_block,
    slot_kind,
    live_count,
):
    bf, f32 = jnp.bfloat16, jnp.float32
    anyspec = pl.BlockSpec(memory_space=pl.ANY)
    smem = pl.BlockSpec(memory_space=pltpu.SMEM)
    dma = pltpu.SemaphoreType.DMA
    grad_x, grad_b = pl.pallas_call(
        kernel,
        out_shape=(
            jax.ShapeDtypeStruct((512, 256), bf),
            jax.ShapeDtypeStruct((SLOTS, 16, TILE), f32),
        ),
        in_specs=[anyspec] * 5 + [smem] * 4,
        out_specs=(anyspec, anyspec),
        scratch_shapes=[
            [pltpu.VMEM((BLOCKS, r, TILE), bf) for r in CHUNKS],
            pltpu.VMEM((16, 256, 768), bf),
            pltpu.VMEM((16, 256, 768), bf),
            pltpu.VMEM((4, 768, 1024), bf),
            pltpu.VMEM((6, max(CHUNKS), TILE), f32),
            pltpu.VMEM((6, max(CHUNKS), TILE), f32),
            pltpu.VMEM((6, max(CHUNKS), TILE), f32),
            [pltpu.VMEM((16, 256, r), bf) for r in CHUNKS],
            [pltpu.VMEM((2, 4, 2, 64, r), bf) for r in CHUNKS],
            [pltpu.VMEM((2, 4, 2, 128, r), bf) for r in CHUNKS],
            [pltpu.VMEM((2, 2, 64, r), bf) for r in CHUNKS],
            [pltpu.VMEM((2, 2, 128, r), bf) for r in CHUNKS],
            pltpu.VMEM((4, SLOTS, TILE, TILE), f32),
            pltpu.VMEM((NC, 16, 8, TILE), f32),
            pltpu.VMEM((NT1, 4, SLOTS, 16, TILE), bf),
            pltpu.VMEM((NT1, 4, SLOTS, 16, TILE), bf),
            pltpu.VMEM((8, TILE), f32),
            pltpu.VMEM((8, TILE), f32),
            pltpu.VMEM((4, SLOTS, 16, TILE), bf),
            pltpu.VMEM((4, SLOTS, 16, TILE), bf),
            dma((NC, 2, 2)),
            dma((6,)),
            dma((NC, 2, 20)),
            dma((NC, 2, 20)),
            dma((NC, 2, 20)),
            dma((NC, 2, 20)),
            dma((NC, 16)),
            dma((NC, 16)),
            dma((NT1,)),
            dma((NT1,)),
            dma((1,)),
            dma((1,)),
            dma((6,)),
            dma((6,)),
            dma((2 * NC + 2,)),
            pltpu.VMEM((512, 256), bf),
            pltpu.VMEM((SLOTS, 16, TILE), f32),
        ],
        compiler_params=pltpu.CompilerParams(
            collective_id=0, has_side_effects=True, vmem_limit_bytes=62 << 20
        ),
        cost_estimate=pl.CostEstimate(
            flops=17_000_000_000, bytes_accessed=20_000_000, transcendentals=400_000
        ),
    )(
        tokens,
        out_grad,
        gate_weight.reshape(16, 256, 768),
        up_weight.reshape(16, 256, 768),
        down_weight,
        slot_ffn_block,
        slot_model_block,
        slot_kind,
        live_count,
    )
    return pl.pallas_call(
        hand_out,
        out_shape=(
            jax.ShapeDtypeStruct((512, 256), bf),
            jax.ShapeDtypeStruct((SLOTS, 16, TILE), f32),
        ),
        in_specs=[anyspec] * 2,
        out_specs=(anyspec, anyspec),
        scratch_shapes=[
            pltpu.VMEM((512, 256), bf),
            pltpu.VMEM((SLOTS, 16, TILE), f32),
            dma((4,)),
        ],
    )(grad_x, grad_b)


def solution(mesh):
    return jax.shard_map(
        per_device,
        mesh=mesh,
        in_specs=(
            P("dp", "tensor"),
            P("dp", "tensor"),
            P(None, "tensor"),
            P(None, "tensor"),
            P("tensor", None),
            P("tensor"),
            P("tensor"),
            P("tensor"),
            P("tensor"),
        ),
        out_specs=(P("dp", "tensor"), P("tensor", "dp", None)),
        check_vma=False,
    )
```
